512 devices in a mesh: seq: 32 (over x, z_hi, core), tensor: 16 (over z_lo, y).
Axes of the slice: x: 4, y: 8, z: 8 (z_hi: 4, z_lo: 2; z = z_hi * 2 + z_lo), core: 2. Of those that a mesh axis runs over, the one named last changes fastest.
Arguments:
- activations: bfloat16 [1, 4096, 4608], P(None, 'seq', 'tensor'), may hold values from -6 to 6
- adapter_down_weight: bfloat16 [4608, 16], P('tensor'), may hold values from -0.09375 to 0.09375
- queries: bfloat16 [1, 4096, 32, 128], P(None, 'seq', 'tensor'), may hold values from -21 to 21
- keys: bfloat16 [1, 4096, 16, 128], P(None, 'seq', 'tensor'), may hold values from -4.5 to 4.5
- values: bfloat16 [1, 4096, 16, 128], P(None, 'seq', 'tensor'), may hold values from -6 to 6
- sequence_lengths: int32 [1], replicated, may hold values from 2048 to 4096
- probe: float32 [4, 16, 32, 128], P(None, None, 'tensor', 'seq'), may hold values from -6 to 6
- basis: float32 [96, 16, 32, 128], P(None, None, 'tensor', 'seq'), may hold values from -6 to 6
Outputs:
- next_block: float32 [1, 4, 16, 32, 128], P(None, None, None, 'tensor', 'seq')
- block_diag: float32 [1, 4, 4], replicated
- block_sub: float32 [1, 4, 4], replicated
The draws below stay inside these ranges and needn't reach their ends.
All inputs are finite; a program needn't handle non-finite values.
Results may differ from the reference program's by a relative error of at most 0.005.
Values may be sent and summed in bfloat16 or wider, within the bound.
A program may use at most 64 MiB of HBM per device.

```python
import math
import jax
import jax.numpy as jnp
from jax import lax

MODEL_WIDTH = 4608
QUERY_HEADS = 32
KEY_VALUE_HEADS = 16
HEAD_WIDTH = 128
ADAPTER_RANK = 16
SEQUENCE_COUNT = 1
PROBE_VECTORS = 4
NB = 96
STEPS = 1
SEQUENCE_LENGTH = 4096


def key_field(key, level):
    first_key, second_key, third_key = jax.random.split(key, 3)
    array_shape = (SEQUENCE_COUNT, SEQUENCE_LENGTH, KEY_VALUE_HEADS, HEAD_WIDTH)
    normal_part = jnp.clip(jax.random.normal(first_key, array_shape, jnp.float32), -4.5, 4.5)
    even_part = jax.random.uniform(second_key, array_shape, jnp.float32, -1.7, 1.7)
    drawn = jnp.where(level > 0, even_part, normal_part)
    signs = jnp.where(jax.random.bernoulli(third_key, 0.5, array_shape), 3.0, -3.0)
    flipper = jnp.where(jnp.arange(HEAD_WIDTH) < HEAD_WIDTH // 2, -1.0, 1.0)
    period = min(256, SEQUENCE_LENGTH)
    marker = period // 2 + 2
    position = jnp.arange(SEQUENCE_LENGTH)[None, :, None, None]
    upper = (position % period == marker - 1) & (level > 0)
    lower_rows = (position % period == marker - 2) & (level > 0)
    shifted = jnp.roll(signs, -1, axis=1) * flipper
    return jnp.where(upper, signs, jnp.where(lower_rows, shifted, drawn))


def draw_keys(key, part):
    level = 0.0
    shared = key_field(key, level)
    return shared.astype(jnp.bfloat16)


def draw_queries(key, part):
    level = 0.0
    shared = key_field(key, level)
    key = jax.random.fold_in(key, 23)
    first_key, second_key = jax.random.split(key)
    array_shape = (SEQUENCE_COUNT, SEQUENCE_LENGTH, QUERY_HEADS, HEAD_WIDTH)
    normal_part = jnp.clip(jax.random.normal(first_key, array_shape, jnp.float32), -4.5, 4.5)
    even_part = jax.random.uniform(second_key, array_shape, jnp.float32, -1.7, 1.7)
    drawn = jnp.where(level > 0, even_part, normal_part)
    query_group_width = QUERY_HEADS // KEY_VALUE_HEADS
    nearer = jnp.repeat(jnp.roll(shared, 1, axis=1), query_group_width, axis=2)
    farther = jnp.repeat(jnp.roll(shared, 2, axis=1), query_group_width, axis=2)
    period = min(256, SEQUENCE_LENGTH)
    marker = period // 2 + 2
    position = jnp.arange(SEQUENCE_LENGTH)[None, :, None, None]
    strength = (1.2 + 0.9 * (position // period % 3)) * 12.6 / math.sqrt(HEAD_WIDTH)
    lesser = strength - 2.0 / (9.0 * math.sqrt(HEAD_WIDTH))
    special = strength * nearer + lesser * farther
    marked = (position % period == marker) & (level > 0)
    return jnp.where(marked, special, drawn).astype(jnp.bfloat16)


def shard_levels(stream_key, shape, cuts, least, largest):
    def one(dim, blocks):
        heights = jax.random.uniform(jax.random.fold_in(jax.random.fold_in(stream_key, 6), dim), (blocks,), jnp.float32, least / len(cuts), largest / len(cuts))
        return jnp.repeat(jnp.exp(heights), shape[dim] // blocks).reshape((-1,) + (1,) * (len(shape) - dim - 1))

    loudness = one(*cuts[0])
    for cut in cuts[1:]:
        loudness = loudness * one(*cut)
    return loudness


def noise(own_key, dims, deviation, reach, shards=(), held_as=jnp.bfloat16):
    drawn = jax.random.normal(own_key, dims, jnp.float32) * deviation
    if len(shards) > 0:
        drawn = shard_levels(own_key, dims, shards, -0.22, 0.18) * drawn
    return jnp.clip(drawn, min=-reach, max=reach).astype(held_as)


def setup_inputs(seed: int = 0) -> dict:
    key_of = jax.random.split(jax.random.key(seed), 9)
    return {
        "activations": noise(key_of[0], (SEQUENCE_COUNT, SEQUENCE_LENGTH, MODEL_WIDTH), 1.0, 6.0, ((1, 32), (2, 16))),
        "adapter_down_weight": noise(key_of[1], (MODEL_WIDTH, ADAPTER_RANK), MODEL_WIDTH ** -0.5, 0.09375, ((0, 16),)),
        "queries": draw_queries(jax.random.fold_in(key_of[8], 71), 0),
        "keys": draw_keys(jax.random.fold_in(key_of[8], 71), 0),
        "values": noise(key_of[4], (SEQUENCE_COUNT, SEQUENCE_LENGTH, KEY_VALUE_HEADS, HEAD_WIDTH), 1.0, 6.0, ((1, 32), (2, 16))),
        "sequence_lengths": jax.random.randint(key_of[5], (SEQUENCE_COUNT,), SEQUENCE_LENGTH // 2, SEQUENCE_LENGTH + 1).astype(jnp.int32),
        "probe": noise(key_of[6], (PROBE_VECTORS, ADAPTER_RANK, QUERY_HEADS, HEAD_WIDTH), 1.0, 6.0, ((2, 16), (3, 32)), jnp.float32),
        "basis": noise(key_of[7], (NB, ADAPTER_RANK, QUERY_HEADS, HEAD_WIDTH), 1.0, 6.0, ((2, 16), (3, 32)), jnp.float32),
    }


adapter_scale = 0.25
query_scale = 144.0 ** (-0.5)
soft_cap = 50.0

def cast_to_bfloat(array):
    return lax.optimization_barrier(array.astype(jnp.bfloat16)).astype(jnp.float32)

def inner_mean(left, right):
    return jnp.dot(left, right.T, precision=lax.Precision.HIGHEST) / (ADAPTER_RANK * QUERY_HEADS * HEAD_WIDTH)

def head_product(head_args, rank_projection, allowed, valid_rows):
    head_q, head_k, head_v, probe_blocks = head_args
    highest_precision = lax.Precision.HIGHEST
    query_full = head_q.astype(jnp.float32)
    key_full = head_k.astype(jnp.float32)
    value_full = head_v.astype(jnp.float32)
    gradient_factor = adapter_scale / (SEQUENCE_COUNT * SEQUENCE_LENGTH)
    raw_scores = query_scale * jnp.einsum('biqd,bjd->bqij', query_full, key_full, precision=highest_precision)
    capped_tanh = jnp.tanh(raw_scores / soft_cap)
    logits = soft_cap * capped_tanh
    cap_slope = 1.0 - capped_tanh * capped_tanh
    key_mask = allowed[:, None]
    run_sum = jnp.sum(jnp.where(key_mask, jnp.exp(logits), 0.0), axis=-1)
    log_norm = jnp.log(run_sum)
    weights = jnp.where(key_mask, jnp.exp(logits - log_norm[..., None]), 0.0)
    sloped = weights * cap_slope
    query_tangent = cast_to_bfloat(adapter_scale * jnp.einsum('swf,afcp->ascwp', rank_projection, probe_blocks, precision=highest_precision))
    tangent_scores = query_scale * jnp.einsum('kbqid,bjd->kbqij', query_tangent, key_full, precision=highest_precision)
    scaled = sloped[None] * tangent_scores
    attended = jnp.einsum('bqij,bjd->bqid', cast_to_bfloat(weights), value_full, precision=highest_precision)
    lifted = jnp.einsum('kbqij,bjd->kbqid', cast_to_bfloat(scaled), value_full, precision=highest_precision)
    weight_sum = jnp.sum(scaled, axis=-1)
    output_tangent = jnp.where(valid_rows[None, :, None, :, None], lifted - weight_sum[..., None] * attended[None], 0.0)
    cotangent = cast_to_bfloat(output_tangent)
    correlation = jnp.sum(output_tangent * attended[None], axis=-1)
    aligned = jnp.einsum('kbqid,bjd->kbqij', cotangent, value_full, precision=highest_precision)
    pushed = sloped[None] * (aligned - correlation[..., None])
    query_grad = query_scale * jnp.einsum('kbqij,bjd->kbqid', cast_to_bfloat(pushed), key_full, precision=highest_precision)
    return gradient_factor * jnp.einsum('bir,kbqid->krqd', rank_projection, query_grad, precision=highest_precision)

def reference(activations, adapter_down_weight, queries, keys, values, sequence_lengths, probe, basis):
    highest_precision = lax.Precision.HIGHEST
    query_group_width = QUERY_HEADS // KEY_VALUE_HEADS
    rank_projection = jnp.dot(activations.reshape(SEQUENCE_COUNT * SEQUENCE_LENGTH, MODEL_WIDTH).astype(jnp.float32), adapter_down_weight.astype(jnp.float32), preferred_element_type=jnp.float32).reshape(SEQUENCE_COUNT, SEQUENCE_LENGTH, ADAPTER_RANK)
    position = jnp.arange(SEQUENCE_LENGTH, dtype=jnp.int32)
    valid_rows = position[None, :] < sequence_lengths[:, None]
    allowed = (position[None, None, :] <= position[None, :, None]) & (position[None, None, :] < sequence_lengths[:, None, None])
    query_heads = queries.reshape(SEQUENCE_COUNT, SEQUENCE_LENGTH, KEY_VALUE_HEADS, query_group_width, HEAD_WIDTH).transpose(2, 0, 1, 3, 4)
    heads_k = keys.transpose(2, 0, 1, 3)
    heads_v = values.transpose(2, 0, 1, 3)
    saved_blocks = [basis.reshape(NB, -1), probe.reshape(PROBE_VECTORS, -1)]
    new_blocks, diag_list, sub_list = ([], [], [])
    for lanczos_step in range(STEPS):
        probe_blocks = saved_blocks[-1].reshape(PROBE_VECTORS, ADAPTER_RANK, KEY_VALUE_HEADS, query_group_width, HEAD_WIDTH).transpose(2, 0, 1, 3, 4)
        grads = lax.map(lambda head_args: head_product(head_args, rank_projection, allowed, valid_rows), (query_heads, heads_k, heads_v, probe_blocks))
        residue = grads.transpose(1, 2, 0, 3, 4).reshape(PROBE_VECTORS, -1)
        stacked = jnp.concatenate(saved_blocks, axis=0)
        coeff_one = inner_mean(stacked, residue)
        diag_list.append(coeff_one[stacked.shape[0] - PROBE_VECTORS:])
        residue = residue - jnp.dot(coeff_one.T, stacked, precision=highest_precision)
        coeff_two = inner_mean(stacked, residue)
        residue = residue - jnp.dot(coeff_two.T, stacked, precision=highest_precision)
        gram = inner_mean(residue, residue)
        factor = jnp.linalg.cholesky(gram)
        next_vector = jax.scipy.linalg.solve_triangular(factor, residue, lower=True)
        sub_list.append(factor.T)
        new_blocks.append(next_vector)
        saved_blocks.append(next_vector)
    next_block = jnp.stack(new_blocks).reshape(STEPS, PROBE_VECTORS, ADAPTER_RANK, QUERY_HEADS, HEAD_WIDTH)
    return (next_block, jnp.stack(diag_list), jnp.stack(sub_list))
```

```python
import functools

import jax
import jax.numpy as jnp
from jax import lax
from jax.experimental import pallas as pl
from jax.experimental.pallas import tpu as pltpu
from jax.sharding import PartitionSpec as P

MESH = pl.DeviceIdType.MESH
HIGHEST = lax.Precision.HIGHEST
F32 = jnp.float32
BF16 = jnp.bfloat16

adapter_scale = 0.25
query_scale = 144.0 ** (-0.5)
soft_cap = 50.0

SEQ = 32
ROWS = 128
WIDTH = 128
RANK = 16
PROBES = 4
NB = 96
KNOWN = NB + PROBES
CHIPS = SEQ // 2
CHUNK = 2 * ROWS
GROUPS = 4
GROUP = ROWS // GROUPS
LANES = 128


def nn(a, b, precision=None):
    return lax.dot_general(
        a, b, (((1,), (0,)), ((), ())), precision=precision, preferred_element_type=F32
    )


def nt(a, b, precision=None):
    return lax.dot_general(
        a, b, (((1,), (1,)), ((), ())), precision=precision, preferred_element_type=F32
    )


def tn(a, b, precision=None):
    return lax.dot_general(
        a, b, (((0,), (0,)), ((), ())), precision=precision, preferred_element_type=F32
    )


def iota(shape, dim):
    return lax.broadcasted_iota(jnp.int32, shape, dim)


def spread(compact):
    lane = iota((PROBES, LANES), 1)
    own = (lane // 32) == iota((PROBES, LANES), 0)
    masked = [
        jnp.where(own, jnp.broadcast_to(compact[d : d + 1], (PROBES, LANES)), 0.0)
        for d in range(4)
    ]
    repeated = []
    for piece in masked:
        piece = piece + pltpu.roll(piece, 32, 1)
        repeated.append(piece + pltpu.roll(piece, 64, 1))
    return jnp.concatenate(masked, axis=1), jnp.concatenate(repeated, axis=1)


def kernel(
    tensor,
    act_hbm,
    down_hbm,
    q_hbm,
    k_hbm,
    v_hbm,
    len_ref,
    probe_hbm,
    basis_hbm,
    next_ref,
    diag_ref,
    sub_ref,
    act,
    down,
    qraw,
    qwide,
    qbuf,
    probe,
    basis,
    kv,
    lhs,
    acc,
    slopes,
    cot,
    corr,
    inv,
    grad,
    vect,
    wbuf,
    srep,
    gmat,
    lr_out,
    lr_in,
    lr,
    vt_out,
    vt_in,
    w_out,
    w_in,
    c_out,
    c_in,
    d_out,
    d_in,
    g_out,
    g_in,
    h_out,
    h_in,
    e_out,
    e_in,
    local_sem,
    kv_send,
    z_recv,
    x_recv,
    sib_recv,
    pair_send,
    pair_recv,
    ex_send,
    ex_recv,
):
    s = lax.axis_index("seq")
    t = lax.axis_index("tensor")
    x, z, core = s // 8, (s // 2) % 4, s % 2
    chip = s // 2
    partner = SEQ - 1 - s
    head = s // (SEQ // 2)

    def seq_at(xx, zz, cc):
        return (lax.rem(xx + 4, 4) * 4 + lax.rem(zz + 4, 4)) * 2 + cc

    loads = [
        pltpu.make_async_copy(src, dst, local_sem.at[i])
        for i, (src, dst) in enumerate(
            (
                (act_hbm, act),
                (down_hbm, down),
                (q_hbm, qraw),
                (probe_hbm, probe),
                (basis_hbm, basis),
                (k_hbm, kv.at[s, 0]),
                (v_hbm, kv.at[s, 1]),
            )
        )
    ]
    for load in loads:
        load.start()

    barrier = pltpu.get_barrier_semaphore()

    def greet_seq(o, carry):
        pl.semaphore_signal(
            barrier, inc=1, device_id={"seq": lax.rem(s + o, SEQ)}, device_id_type=MESH
        )
        return carry

    def greet_tensor(o, carry):
        pl.semaphore_signal(
            barrier,
            inc=1,
            device_id={"tensor": lax.rem(t + o, tensor)},
            device_id_type=MESH,
        )
        return carry

    lax.fori_loop(1, SEQ, greet_seq, 0)
    lax.fori_loop(1, tensor, greet_tensor, 0)
    pl.semaphore_wait(barrier, SEQ - 1 + tensor - 1)

    def send_seq(src_of, into, n):
        def body(o, carry):
            to = lax.rem(s + o, SEQ)
            pltpu.make_async_remote_copy(
                src_ref=src_of(to),
                dst_ref=into.at[s],
                send_sem=ex_send.at[n],
                recv_sem=ex_recv.at[n],
                device_id={"seq": to},
                device_id_type=MESH,
            ).start()
            return carry

        lax.fori_loop(1, SEQ, body, 0)

    def send_tensor(src, into, n):
        def body(o, carry):
            pltpu.make_async_remote_copy(
                src_ref=src,
                dst_ref=into.at[t],
                send_sem=ex_send.at[n],
                recv_sem=ex_recv.at[n],
                device_id={"tensor": lax.rem(t + o, tensor)},
                device_id_type=MESH,
            ).start()
            return carry

        lax.fori_loop(1, tensor, body, 0)

    def arrived(into, n):
        span = into.at[pl.ds(0, into.shape[0] - 1)]
        pltpu.make_async_copy(span, span, ex_recv.at[n]).wait()

    def sent(into, n):
        span = into.at[pl.ds(0, into.shape[0] - 1)]
        pltpu.make_async_copy(span, span, ex_send.at[n]).wait()

    def total(into):
        out = into[0]
        for i in range(1, into.shape[0]):
            out = out + into[i]
        return out

    def push(src, to, sem):
        pltpu.make_async_remote_copy(
            src_ref=src,
            dst_ref=src,
            send_sem=kv_send,
            recv_sem=sem,
            device_id={"seq": to},
            device_id_type=MESH,
        ).start()

    def came(ref, sem):
        pltpu.make_async_copy(ref, ref, sem).wait()

    z_up, z_down = seq_at(x, z + 1, core), seq_at(x, z + 3, core)
    x_up, x_down = seq_at(x + 1, z, core), seq_at(x + 3, z, core)
    sibling = seq_at(x, z, 1 - core)

    def push_column(d):
        src = kv.at[seq_at(x, z + d, core)]
        push(src, x_up, x_recv.at[d, 0])
        push(src, x_down, x_recv.at[d, 1])
        push(src, sibling, sib_recv.at[0, d])

    def pass_x(d):
        below = seq_at(x + 3, z + d, core)
        came(kv.at[below], x_recv.at[d, 0])
        push(kv.at[below, 0], x_up, x_recv.at[d, 2])
        push(kv.at[below], sibling, sib_recv.at[3, d])
        above = seq_at(x + 1, z + d, core)
        came(kv.at[above], x_recv.at[d, 1])
        push(kv.at[above, 1], x_down, x_recv.at[d, 3])
        push(kv.at[above], sibling, sib_recv.at[1, d])

    def pass_far(d):
        far = seq_at(x + 2, z + d, core)
        came(kv.at[far, 0], x_recv.at[d, 2])
        came(kv.at[far, 1], x_recv.at[d, 3])
        push(kv.at[far], sibling, sib_recv.at[2, d])

    loads[5].wait()
    loads[6].wait()
    mine = kv.at[s]
    push(mine, z_up, z_recv.at[0])
    push(mine, z_down, z_recv.at[1])
    push_column(0)

    loads[0].wait()
    loads[1].wait()
    partial = nn(down[...], act[...])
    lr_out[...] = partial
    lr_in[t] = partial
    send_tensor(lr_out, lr_in, 0)

    loads[3].wait()
    compact = jnp.concatenate(
        [probe[k, h] for k in range(PROBES) for h in range(2)], axis=1
    )
    vt_out[...] = compact
    vt_in[s] = compact
    send_seq(lambda to: vt_out, vt_in, 1)

    loads[2].wait()
    qwide[...] = qraw[...].astype(F32)
    qbuf[0] = qwide[pl.ds(head, ROWS, stride=2), :].astype(BF16)
    qbuf[2] = qwide[pl.ds(1 - head, ROWS, stride=2), :].astype(BF16)
    q_copy = pltpu.make_async_remote_copy(
        src_ref=qbuf.at[2],
        dst_ref=qbuf.at[1],
        send_sem=pair_send.at[0],
        recv_sem=pair_recv.at[0],
        device_id={"seq": partner},
        device_id_type=MESH,
    )
    q_copy.start()

    loads[4].wait()
    inner = iota((LANES, 4 * LANES), 0)
    outer = iota((LANES, 4 * LANES), 1)
    place = (
        (inner // 8 == outer % 16)
        & ((inner // 4) % 2 == (outer // 16) % 2)
        & (inner % 4 == outer // LANES)
    )
    srep[...] = jnp.zeros((LANES, 4 * LANES), F32)
    srep[0:NB] = tn(basis[...], place.astype(F32), HIGHEST)
    srep[NB:KNOWN] = spread(compact)[1]
    kinds = srep[...]
    gram = nt(kinds[:, :], kinds[:, :], HIGHEST) * (0.25 / (RANK * 2 * tensor * WIDTH))
    for i in range(SEQ):
        g_out[i] = gram[4 * i : 4 * i + 4]
    g_in[s] = g_out[s]
    send_seq(lambda to: g_out.at[to], g_in, 2)

    below = seq_at(x, z + 3, core)
    came(kv.at[below], z_recv.at[0])
    push(kv.at[below, 0], z_up, z_recv.at[2])
    push_column(3)
    above = seq_at(x, z + 1, core)
    came(kv.at[above], z_recv.at[1])
    push(kv.at[above, 1], z_down, z_recv.at[3])
    push_column(1)
    pass_x(0)
    far = seq_at(x, z + 2, core)
    came(kv.at[far, 0], z_recv.at[2])
    came(kv.at[far, 1], z_recv.at[3])
    push_column(2)

    arrived(lr_in, 0)
    lr[0] = total(lr_in)
    lr_copy = pltpu.make_async_remote_copy(
        src_ref=lr.at[0],
        dst_ref=lr.at[1],
        send_sem=pair_send.at[1],
        recv_sem=pair_recv.at[1],
        device_id={"seq": partner},
        device_id_type=MESH,
    )
    lr_copy.start()

    arrived(vt_in, 1)
    vect[...] = jnp.concatenate([vt_in[i] for i in range(SEQ)], axis=0).T
    q_copy.wait_recv()
    lr_copy.wait_recv()
    for b in range(2):
        for g in range(GROUPS):
            rows = pl.ds(g * GROUP, GROUP)
            lhs[b, g, 0:GROUP] = qbuf[b, rows]
        low = lr[b]
        for k in range(PROBES):
            vk = vect[pl.ds(pl.multiple_of(k * 32 + head * 16, 16), RANK), :]
            tangent = (adapter_scale * tn(low, vk, HIGHEST)).astype(BF16)
            for g in range(GROUPS):
                lhs[b, g, (k + 1) * GROUP : (k + 2) * GROUP] = tangent[
                    g * GROUP : (g + 1) * GROUP
                ]

    acc[...] = jnp.zeros(acc.shape, F32)
    ones = jnp.ones((CHUNK, WIDTH), BF16)
    length = len_ref[0]

    def first_of(b):
        return jnp.where(b == 0, s, partner) * ROWS

    def last_chunk(b):
        return jnp.where(b == 0, s, partner) // 2

    def keys_of(c):
        return jnp.concatenate([kv[2 * c, 0], kv[2 * c + 1, 0]], axis=0)

    def values_of(c):
        return jnp.concatenate([kv[2 * c, 1], kv[2 * c + 1, 1]], axis=0)

    def first_pass(b, c):
        keys = keys_of(c)
        ext = jnp.concatenate([values_of(c), ones], axis=1)
        for g in range(GROUPS):
            scores = nt(lhs[b, g], keys)
            capped = jnp.tanh(scores[0:GROUP] * (query_scale / soft_cap))
            row = first_of(b) + g * GROUP + iota((GROUP, 1), 0)
            limit = jnp.minimum(row, length - 1) - c * CHUNK
            weights = jnp.where(
                iota((GROUP, CHUNK), 1) <= limit, jnp.exp(soft_cap * capped), 0.0
            )
            sloped = weights * (1.0 - capped * capped)
            slopes[b, c, g] = sloped
            high = weights.astype(BF16)
            parts = [high, (weights - high.astype(F32)).astype(BF16)]
            for k in range(PROBES):
                parts.append(
                    (sloped * scores[(k + 1) * GROUP : (k + 2) * GROUP]).astype(BF16)
                )
            acc[b, g] += nn(jnp.concatenate(parts, axis=0), ext)

    def order(i):
        return jnp.where(i == 0, 0, jnp.where(i == 1, 3, i - 1))

    def column_step(p, carry):
        d = order(p)

        @pl.when(p > 0)
        def _():
            pass_x(d)

        def chunk_step(q, carry):
            e = order(q)

            @pl.when(q == 3)
            def _():
                pass_far(d)

            other = seq_at(x + e, z + d, 1 - core)
            came(kv.at[other], sib_recv.at[e, d])
            c = other // 2

            def block_step(b, carry):
                @pl.when(c <= last_chunk(b))
                def _():
                    first_pass(b, c)

                return carry

            return lax.fori_loop(0, 2, block_step, carry)

        return lax.fori_loop(0, 4, chunk_step, carry)

    lax.fori_loop(0, 4, column_step, 0)

    arrived(g_in, 2)
    piece = total(g_in)
    h_out[...] = piece
    h_in[t] = piece
    send_tensor(h_out, h_in, 3)

    def turn(b, carry):
        for g in range(GROUPS):
            full = acc[b, g]
            plain = full[0:GROUP] + full[GROUP : 2 * GROUP]
            share = 1.0 / plain[:, WIDTH:]
            attended = plain[:, :WIDTH] * share
            share_scaled = share * query_scale
            row = first_of(b) + g * GROUP + iota((GROUP, 1), 0)
            valid = row < length
            for k in range(PROBES):
                part = full[(k + 2) * GROUP : (k + 3) * GROUP]
                tangent = (part[:, :WIDTH] - part[:, WIDTH:] * attended) * share_scaled
                tangent = jnp.where(valid, tangent, 0.0)
                cot[b, g, k * GROUP : (k + 1) * GROUP] = tangent.astype(BF16)
                corr[b, g, k * GROUP : (k + 1) * GROUP] = jnp.broadcast_to(
                    jnp.sum(tangent * attended, axis=1, keepdims=True), (GROUP, WIDTH)
                )
            inv[b, g] = share * (query_scale * adapter_scale / (SEQ * ROWS))
        return carry

    lax.fori_loop(0, 2, turn, 0)

    grad[...] = jnp.zeros(grad.shape, F32)

    def second_pass(b, c):
        keys = keys_of(c)
        values = values_of(c)
        for g in range(GROUPS):
            aligned = nt(cot[b, g], values)
            sloped = slopes[b, c, g]
            parts = []
            for k in range(PROBES):
                level = corr[b, g, k * GROUP : (k + 1) * GROUP]
                level = jnp.concatenate([level, level], axis=1)
                parts.append(
                    (sloped * (aligned[k * GROUP : (k + 1) * GROUP] - level)).astype(
                        BF16
                    )
                )
            grad[b, g] += nn(jnp.concatenate(parts, axis=0), keys)

    def second_block(b, carry):
        def step(c, carry):
            second_pass(b, c)
            return carry

        return lax.fori_loop(0, last_chunk(b) + 1, step, carry)

    lax.fori_loop(0, 2, second_block, 0)

    wbuf[...] = jnp.zeros((LANES, WIDTH), F32)
    both = jnp.concatenate([lr[0], lr[1]], axis=1)
    for k in range(PROBES):
        stack = jnp.concatenate(
            [
                grad[b, g, k * GROUP : (k + 1) * GROUP] * inv[b, g]
                for b in range(2)
                for g in range(GROUPS)
            ],
            axis=0,
        )
        wbuf[pl.ds(pl.multiple_of(k * 32 + head * 16, 16), RANK), :] = nn(
            both, stack, HIGHEST
        )
    turned = wbuf[...].T
    for i in range(SEQ):
        w_out[i] = turned[4 * i : 4 * i + 4]
    w_in[s] = w_out[s]
    send_seq(lambda to: w_out.at[to], w_in, 4)

    arrived(h_in, 3)
    piece = total(h_in)
    e_out[...] = piece
    e_in[s] = piece
    send_seq(lambda to: e_out, e_in, 5)

    arrived(w_in, 4)
    masked, repeated = spread(total(w_in))
    srep[KNOWN : KNOWN + PROBES] = repeated
    dots = nt(masked, srep[...], HIGHEST) * (1.0 / (RANK * 2 * tensor * WIDTH))
    c_out[...] = dots
    c_in[s] = dots
    send_seq(lambda to: c_out, c_in, 6)

    arrived(e_in, 5)
    gmat[...] = jnp.concatenate([e_in[i] for i in range(SEQ)], axis=0)
    gfull = gmat[...]
    eye = (iota((LANES, LANES), 0) == iota((LANES, LANES), 1)).astype(F32)
    square = nn(gfull, gfull, HIGHEST)
    cube = nn(square, gfull, HIGHEST)
    once = 2.0 * eye - gfull
    twice = 4.0 * (eye + square) - 6.0 * gfull - cube

    arrived(c_in, 6)
    piece = total(c_in)
    d_out[...] = piece
    d_in[t] = piece
    send_tensor(d_out, d_in, 7)
    arrived(d_in, 7)
    dots = total(d_in)

    lane = iota((PROBES, LANES), 1)
    known = jnp.where(lane < KNOWN, dots, 0.0)
    coeff = nn(known, once, HIGHEST)
    quad = nn(known, twice, HIGHEST)
    pick = (lane == iota((PROBES, LANES), 0) + NB).astype(F32)
    small = nt(jnp.concatenate([quad, pick], axis=0), known, HIGHEST)
    gram = dots[:, KNOWN : KNOWN + PROBES] - small[0:PROBES]
    diag_ref[0] = small[PROBES:]

    low = [[None] * PROBES for _ in range(PROBES)]
    for j in range(PROBES):
        pivot = gram[j : j + 1, j : j + 1]
        for m in range(j):
            pivot = pivot - low[j][m] * low[j][m]
        low[j][j] = jnp.sqrt(pivot)
        for i in range(j + 1, PROBES):
            entry = gram[i : i + 1, j : j + 1]
            for m in range(j):
                entry = entry - low[i][m] * low[j][m]
            low[i][j] = entry / low[j][j]
    row4, col4 = iota((PROBES, PROBES), 0), iota((PROBES, PROBES), 1)
    upper = jnp.zeros((PROBES, PROBES), F32)
    for i in range(PROBES):
        for j in range(i + 1):
            upper = jnp.where((row4 == j) & (col4 == i), low[i][j], upper)
    sub_ref[0] = upper

    mix = jnp.where(
        lane < KNOWN,
        -coeff,
        (lane == iota((PROBES, LANES), 0) + KNOWN).astype(F32),
    )
    residue = nn(mix, srep[...], HIGHEST)
    rows = []
    for i in range(PROBES):
        row = residue[i : i + 1]
        for m in range(i):
            row = row - low[i][m] * rows[m]
        rows.append(row / low[i][i])
    lane1 = iota((1, LANES), 1) // 32
    made = []
    for d in range(4):
        row = rows[0][:, d * LANES : (d + 1) * LANES]
        for k in range(1, PROBES):
            row = jnp.where(lane1 == k, rows[k][:, d * LANES : (d + 1) * LANES], row)
        made.append(row)
    made = jnp.concatenate(made, axis=0)
    for k in range(PROBES):
        for h in range(2):
            at = k * 32 + h * 16
            next_ref[k, h] = made[:, at : at + 16]

    shards = kv.at[pl.ds(0, SEQ - 1)]
    pltpu.make_async_copy(shards, shards, kv_send).wait()
    q_copy.wait_send()
    lr_copy.wait_send()
    for n, into in enumerate((lr_in, vt_in, g_in, h_in, w_in, e_in, c_in, d_in)):
        sent(into, n)


def on_device(
    activations, adapter_down_weight, queries, keys, values, sequence_lengths, probe, basis
):
    tensor = lax.axis_size("tensor")
    width = activations.shape[2]
    act = activations.reshape(ROWS, width).T
    down = adapter_down_weight.T
    q = queries.reshape(2 * ROWS, WIDTH)
    k = keys.reshape(ROWS, WIDTH)
    v = values.reshape(ROWS, WIDTH)
    probe_in = probe.transpose(0, 2, 3, 1)
    basis_in = basis.transpose(1, 2, 3, 0).reshape(LANES, NB)
    anywhere = pl.BlockSpec(memory_space=pl.ANY)
    in_vmem = pl.BlockSpec(memory_space=pltpu.VMEM)
    piece = (4, LANES)
    by_seq = pltpu.VMEM((SEQ,) + piece, F32)
    by_tensor = pltpu.VMEM((tensor,) + piece, F32)
    one = pltpu.VMEM(piece, F32)
    turned, diag, sub = pl.pallas_call(
        functools.partial(kernel, tensor),
        out_shape=(
            jax.ShapeDtypeStruct((PROBES, 2, 4, RANK), F32),
            jax.ShapeDtypeStruct((1, PROBES, PROBES), F32),
            jax.ShapeDtypeStruct((1, PROBES, PROBES), F32),
        ),
        in_specs=[anywhere] * 5
        + [pl.BlockSpec(memory_space=pltpu.SMEM)]
        + [anywhere] * 2,
        out_specs=(in_vmem,) * 3,
        scratch_shapes=[
            pltpu.VMEM((width, ROWS), BF16),
            pltpu.VMEM((RANK, width), BF16),
            pltpu.VMEM((2 * ROWS, WIDTH), BF16),
            pltpu.VMEM((2 * ROWS, WIDTH), F32),
            pltpu.VMEM((3, ROWS, WIDTH), BF16),
            pltpu.VMEM((PROBES, 2, 4, RANK), F32),
            pltpu.VMEM((LANES, NB), F32),
            pltpu.VMEM((SEQ, 2, ROWS, WIDTH), BF16),
            pltpu.VMEM((2, GROUPS, (PROBES + 1) * GROUP, WIDTH), BF16),
            pltpu.VMEM((2, GROUPS, (PROBES + 2) * GROUP, 2 * WIDTH), F32),
            pltpu.VMEM((2, CHIPS, GROUPS, GROUP, CHUNK), F32),
            pltpu.VMEM((2, GROUPS, PROBES * GROUP, WIDTH), BF16),
            pltpu.VMEM((2, GROUPS, PROBES * GROUP, WIDTH), F32),
            pltpu.VMEM((2, GROUPS, GROUP, WIDTH), F32),
            pltpu.VMEM((2, GROUPS, PROBES * GROUP, WIDTH), F32),
            pltpu.VMEM((LANES, WIDTH), F32),
            pltpu.VMEM((LANES, WIDTH), F32),
            pltpu.VMEM((LANES, 4 * LANES), F32),
            pltpu.VMEM((LANES, LANES), F32),
            pltpu.VMEM((RANK, ROWS), F32),
            pltpu.VMEM((tensor, RANK, ROWS), F32),
            pltpu.VMEM((2, RANK, ROWS), F32),
            one,
            by_seq,
            by_seq,
            by_seq,
            one,
            by_seq,
            one,
            by_tensor,
            by_seq,
            by_seq,
            one,
            by_tensor,
            one,
            by_seq,
            pltpu.SemaphoreType.DMA((7,)),
            pltpu.SemaphoreType.DMA,
            pltpu.SemaphoreType.DMA((4,)),
            pltpu.SemaphoreType.DMA((4, 4)),
            pltpu.SemaphoreType.DMA((4, 4)),
            pltpu.SemaphoreType.DMA((2,)),
            pltpu.SemaphoreType.DMA((2,)),
            pltpu.SemaphoreType.DMA((8,)),
            pltpu.SemaphoreType.DMA((8,)),
        ],
        compiler_params=pltpu.CompilerParams(
            collective_id=0, has_side_effects=True, vmem_limit_bytes=40 * 1024 * 1024
        ),
    )(act, down, q, k, v, sequence_lengths, probe_in, basis_in)
    return turned.transpose(0, 3, 1, 2)[None], diag, sub


def solution(mesh):
    in_specs = (
        P(None, "seq", "tensor"),
        P("tensor", None),
        P(None, "seq", "tensor", None),
        P(None, "seq", "tensor", None),
        P(None, "seq", "tensor", None),
        P(),
        P(None, None, "tensor", "seq"),
        P(None, None, "tensor", "seq"),
    )
    out_specs = (P(None, None, None, "tensor", "seq"), P(), P())
    return jax.shard_map(
        on_device, mesh=mesh, in_specs=in_specs, out_specs=out_specs, check_vma=False
    )
```

```python
import functools

import jax
import jax.numpy as jnp
from jax import lax
from jax.experimental import pallas as pl
from jax.experimental.pallas import tpu as pltpu
from jax.sharding import PartitionSpec as P

MESH = pl.DeviceIdType.MESH
HIGHEST = lax.Precision.HIGHEST
F32 = jnp.float32
BF16 = jnp.bfloat16

adapter_scale = 0.25
query_scale = 144.0 ** (-0.5)
soft_cap = 50.0

SEQ = 32
ROWS = 128
WIDTH = 128
RANK = 16
PROBES = 4
NB = 96
KNOWN = NB + PROBES
CHUNK = 4 * ROWS
CHUNKS = SEQ // 4
GROUPS = 2
GROUP = ROWS // GROUPS
LANES = 128


def nn(a, b, precision=None):
    return lax.dot_general(
        a, b, (((1,), (0,)), ((), ())), precision=precision, preferred_element_type=F32
    )


def nt(a, b, precision=None):
    return lax.dot_general(
        a, b, (((1,), (1,)), ((), ())), precision=precision, preferred_element_type=F32
    )


def tn(a, b, precision=None):
    return lax.dot_general(
        a, b, (((0,), (0,)), ((), ())), precision=precision, preferred_element_type=F32
    )


def iota(shape, dim):
    return lax.broadcasted_iota(jnp.int32, shape, dim)


def spread(compact):
    lane = iota((PROBES, LANES), 1)
    own = (lane // 32) == iota((PROBES, LANES), 0)
    masked = [
        jnp.where(own, jnp.broadcast_to(compact[d : d + 1], (PROBES, LANES)), 0.0)
        for d in range(4)
    ]
    repeated = []
    for piece in masked:
        piece = piece + pltpu.roll(piece, 32, 1)
        repeated.append(piece + pltpu.roll(piece, 64, 1))
    return jnp.concatenate(masked, axis=1), jnp.concatenate(repeated, axis=1)


def kernel(
    tensor,
    act_hbm,
    down_hbm,
    q_hbm,
    k_hbm,
    v_hbm,
    len_ref,
    probe_hbm,
    basis_hbm,
    out_ref,
    act,
    down,
    qraw,
    qwide,
    qbuf,
    probe,
    basis,
    kv,
    lhs,
    acc,
    slopes,
    cot,
    corr,
    inv,
    grad,
    vect,
    wbuf,
    srep,
    gmat,
    lr_out,
    lr_in,
    lr,
    vt_out,
    vt_in,
    w_out,
    w_in,
    c_out,
    c_in,
    d_out,
    d_in,
    g_out,
    g_in,
    h_out,
    h_in,
    e_out,
    e_in,
    local_sem,
    kv_send,
    z_recv,
    x_recv,
    sib_recv,
    pair_send,
    pair_recv,
    ex_send,
    ex_recv,
):
    s = lax.axis_index("seq")
    t = lax.axis_index("tensor")
    x, z, core = s // 8, (s // 2) % 4, s % 2
    partner = SEQ - 1 - s
    head = s // (SEQ // 2)

    def seq_at(xx, zz, cc):
        return (lax.rem(xx + 4, 4) * 4 + lax.rem(zz + 4, 4)) * 2 + cc

    loads = [
        pltpu.make_async_copy(src, dst, local_sem.at[i])
        for i, (src, dst) in enumerate(
            (
                (act_hbm, act),
                (down_hbm, down),
                (q_hbm, qraw),
                (probe_hbm, probe),
                (basis_hbm, basis),
                (k_hbm, kv.at[s, 0]),
                (v_hbm, kv.at[s, 1]),
            )
        )
    ]
    for load in loads:
        load.start()

    barrier = pltpu.get_barrier_semaphore()

    def greet_seq(o, carry):
        pl.semaphore_signal(
            barrier, inc=1, device_id={"seq": lax.rem(s + o, SEQ)}, device_id_type=MESH
        )
        return carry

    def greet_tensor(o, carry):
        pl.semaphore_signal(
            barrier,
            inc=1,
            device_id={"tensor": lax.rem(t + o, tensor)},
            device_id_type=MESH,
        )
        return carry

    lax.fori_loop(1, SEQ, greet_seq, 0)
    lax.fori_loop(1, tensor, greet_tensor, 0)

    def send_seq(src_of, into, n):
        def body(o, carry):
            to = lax.rem(s + o, SEQ)
            pltpu.make_async_remote_copy(
                src_ref=src_of(to),
                dst_ref=into.at[s],
                send_sem=ex_send.at[n],
                recv_sem=ex_recv.at[n],
                device_id={"seq": to},
                device_id_type=MESH,
            ).start()
            return carry

        lax.fori_loop(1, SEQ, body, 0)

    def send_tensor(src, into, n):
        def body(o, carry):
            pltpu.make_async_remote_copy(
                src_ref=src,
                dst_ref=into.at[t],
                send_sem=ex_send.at[n],
                recv_sem=ex_recv.at[n],
                device_id={"tensor": lax.rem(t + o, tensor)},
                device_id_type=MESH,
            ).start()
            return carry

        lax.fori_loop(1, tensor, body, 0)

    def arrived(into, n):
        span = into.at[pl.ds(0, into.shape[0] - 1)]
        pltpu.make_async_copy(span, span, ex_recv.at[n]).wait()

    def sent(into, n):
        span = into.at[pl.ds(0, into.shape[0] - 1)]
        pltpu.make_async_copy(span, span, ex_send.at[n]).wait()

    def total(into):
        out = into[0]
        for i in range(1, into.shape[0]):
            out = out + into[i]
        return out

    def push(src, to, sem):
        pltpu.make_async_remote_copy(
            src_ref=src,
            dst_ref=src,
            send_sem=kv_send,
            recv_sem=sem,
            device_id={"seq": to},
            device_id_type=MESH,
        ).start()

    def came(ref, sem):
        pltpu.make_async_copy(ref, ref, sem).wait()

    z_up, z_down = seq_at(x, z + 1, core), seq_at(x, z + 3, core)
    x_up, x_down = seq_at(x + 1, z, core), seq_at(x + 3, z, core)
    sibling = seq_at(x, z, 1 - core)

    def push_column(d):
        src = kv.at[seq_at(x, z + d, core)]
        push(src, x_up, x_recv.at[d, 0])
        push(src, x_down, x_recv.at[d, 1])
        push(src, sibling, sib_recv.at[0, d])

    def pass_x(d):
        below = seq_at(x + 3, z + d, core)
        came(kv.at[below], x_recv.at[d, 0])
        push(kv.at[below, 0], x_up, x_recv.at[d, 2])
        push(kv.at[below], sibling, sib_recv.at[3, d])
        above = seq_at(x + 1, z + d, core)
        came(kv.at[above], x_recv.at[d, 1])
        push(kv.at[above, 1], x_down, x_recv.at[d, 3])
        push(kv.at[above], sibling, sib_recv.at[1, d])

    def pass_far(d):
        far = seq_at(x + 2, z + d, core)
        came(kv.at[far, 0], x_recv.at[d, 2])
        came(kv.at[far, 1], x_recv.at[d, 3])
        push(kv.at[far], sibling, sib_recv.at[2, d])

    loads[0].wait()
    loads[1].wait()
    partial = nn(down[...], act[...])
    lr_out[...] = partial
    lr_in[t] = partial

    loads[3].wait()
    compact = jnp.concatenate(
        [probe[k, h] for k in range(PROBES) for h in range(2)], axis=1
    )
    vt_out[...] = compact
    vt_in[s] = compact

    loads[2].wait()
    qwide[...] = qraw[...].astype(F32)
    qbuf[0] = qwide[pl.ds(head, ROWS, stride=2), :].astype(BF16)
    qbuf[2] = qwide[pl.ds(1 - head, ROWS, stride=2), :].astype(BF16)

    loads[4].wait()
    inner = iota((LANES, 4 * LANES), 0)
    outer = iota((LANES, 4 * LANES), 1)
    place = (
        (inner // 8 == outer % 16)
        & ((inner // 4) % 2 == (outer // 16) % 2)
        & (inner % 4 == outer // LANES)
    )
    srep[...] = jnp.zeros((LANES, 4 * LANES), F32)
    srep[0:NB] = tn(basis[...], place.astype(F32), HIGHEST)
    srep[NB:KNOWN] = spread(compact)[1]
    kinds = srep[...]
    gram = nt(kinds, kinds, HIGHEST) * (0.25 / (RANK * 2 * tensor * WIDTH))
    for i in range(SEQ):
        g_out[i] = gram[4 * i : 4 * i + 4]
    g_in[s] = g_out[s]
    loads[5].wait()
    loads[6].wait()

    pl.semaphore_wait(barrier, SEQ - 1 + tensor - 1)
    mine = kv.at[s]
    push(mine, z_up, z_recv.at[0])
    push(mine, z_down, z_recv.at[1])
    push_column(0)
    send_tensor(lr_out, lr_in, 0)
    send_seq(lambda to: vt_out, vt_in, 1)
    q_copy = pltpu.make_async_remote_copy(
        src_ref=qbuf.at[2],
        dst_ref=qbuf.at[1],
        send_sem=pair_send.at[0],
        recv_sem=pair_recv.at[0],
        device_id={"seq": partner},
        device_id_type=MESH,
    )
    q_copy.start()

    below = seq_at(x, z + 3, core)
    came(kv.at[below], z_recv.at[0])
    push(kv.at[below, 0], z_up, z_recv.at[2])
    push_column(3)
    above = seq_at(x, z + 1, core)
    came(kv.at[above], z_recv.at[1])
    push(kv.at[above, 1], z_down, z_recv.at[3])
    push_column(1)
    pass_x(0)

    arrived(lr_in, 0)
    lr[0] = total(lr_in)
    lr_copy = pltpu.make_async_remote_copy(
        src_ref=lr.at[0],
        dst_ref=lr.at[1],
        send_sem=pair_send.at[1],
        recv_sem=pair_recv.at[1],
        device_id={"seq": partner},
        device_id_type=MESH,
    )
    lr_copy.start()

    far = seq_at(x, z + 2, core)
    came(kv.at[far, 0], z_recv.at[2])
    came(kv.at[far, 1], z_recv.at[3])
    push_column(2)
    pass_far(0)
    pass_x(3)
    pass_x(1)

    arrived(vt_in, 1)
    vect[...] = jnp.concatenate([vt_in[i] for i in range(SEQ)], axis=0).T

    def left_side(b):
        low = lr[b]
        query = qbuf[b]
        for g in range(GROUPS):
            lhs[b, g, 0:GROUP] = query[g * GROUP : (g + 1) * GROUP]
        for k in range(PROBES):
            vk = vect[pl.ds(pl.multiple_of(k * 32 + head * 16, 16), RANK), :]
            tangent = (adapter_scale * tn(low, vk, HIGHEST)).astype(BF16)
            for g in range(GROUPS):
                lhs[b, g, (k + 1) * GROUP : (k + 2) * GROUP] = tangent[
                    g * GROUP : (g + 1) * GROUP
                ]

    left_side(0)
    send_seq(lambda to: g_out.at[to], g_in, 2)
    q_copy.wait_recv()
    lr_copy.wait_recv()
    left_side(1)

    acc[...] = jnp.zeros(acc.shape, F32)
    ones = jnp.ones((CHUNK, WIDTH), BF16)
    length = len_ref[0]

    def first_of(b):
        return jnp.where(b == 0, s, partner) * ROWS

    def last_chunk(b):
        return jnp.where(b == 0, s, partner) // 4

    def keys_of(c):
        return jnp.concatenate([kv[4 * c + i, 0] for i in range(4)], axis=0)

    def values_of(c):
        return jnp.concatenate([kv[4 * c + i, 1] for i in range(4)], axis=0)

    def first_pass(b, c):
        keys = keys_of(c)
        ext = jnp.concatenate([values_of(c), ones], axis=1)
        for g in range(GROUPS):
            scores = nt(lhs[b, g], keys)
            capped = jnp.tanh(scores[0:GROUP] * (query_scale / soft_cap))
            row = first_of(b) + g * GROUP + iota((GROUP, 1), 0)
            limit = jnp.minimum(row, length - 1) - c * CHUNK
            weights = jnp.where(
                iota((GROUP, CHUNK), 1) <= limit, jnp.exp(soft_cap * capped), 0.0
            )
            sloped = weights * (1.0 - capped * capped)
            slopes[b, c, g * GROUP : (g + 1) * GROUP] = sloped
            high = weights.astype(BF16)
            parts = [high, (weights - high.astype(F32)).astype(BF16)]
            for k in range(PROBES):
                parts.append(
                    (sloped * scores[(k + 1) * GROUP : (k + 2) * GROUP]).astype(BF16)
                )
            acc[b, g] += nn(jnp.concatenate(parts, axis=0), ext)

    def column_step(q, carry):
        e = jnp.where(q == 0, 0, jnp.where(q == 1, 3, q - 1))

        @pl.when(q == 1)
        def _():
            pass_x(2)
            pass_far(3)
            pass_far(1)

        @pl.when(q == 3)
        def _():
            pass_far(2)

        def pair_step(p, carry):
            pair = lax.rem(z // 2 + p, 2)
            for i in range(2):
                other = seq_at(x + e, 2 * pair + i, 1 - core)
                came(kv.at[other], sib_recv.at[e, lax.rem(2 * pair + i - z + 4, 4)])
            c = seq_at(x + e, 2 * pair, 0) // 4

            def block_step(b, carry):
                @pl.when(c <= last_chunk(b))
                def _():
                    first_pass(b, c)

                return carry

            return lax.fori_loop(0, 2, block_step, carry)

        return lax.fori_loop(0, 2, pair_step, carry)

    lax.fori_loop(0, 4, column_step, 0)

    arrived(g_in, 2)
    piece = total(g_in)
    h_out[...] = piece
    h_in[t] = piece
    send_tensor(h_out, h_in, 3)

    def turn(b, carry):
        for g in range(GROUPS):
            full = acc[b, g]
            plain = full[0:GROUP] + full[GROUP : 2 * GROUP]
            share = 1.0 / plain[:, WIDTH:]
            attended = plain[:, :WIDTH] * share
            share_scaled = share * query_scale
            row = first_of(b) + g * GROUP + iota((GROUP, 1), 0)
            valid = row < length
            for k in range(PROBES):
                part = full[(k + 2) * GROUP : (k + 3) * GROUP]
                tangent = (part[:, :WIDTH] - part[:, WIDTH:] * attended) * share_scaled
                tangent = jnp.where(valid, tangent, 0.0)
                at = k * ROWS + g * GROUP
                cot[b, at : at + GROUP] = tangent.astype(BF16)
                corr[b, at : at + GROUP] = jnp.broadcast_to(
                    jnp.sum(tangent * attended, axis=1, keepdims=True), (GROUP, WIDTH)
                )
            inv[b, g * GROUP : (g + 1) * GROUP] = share * (
                query_scale * adapter_scale / (SEQ * ROWS)
            )
        return carry

    lax.fori_loop(0, 2, turn, 0)

    grad[...] = jnp.zeros(grad.shape, F32)

    def second_pass(b, c):
        aligned = nt(cot[b], values_of(c))
        sloped = slopes[b, c]
        parts = []
        for k in range(PROBES):
            level = corr[b, k * ROWS : (k + 1) * ROWS]
            level = jnp.concatenate([level] * (CHUNK // WIDTH), axis=1)
            parts.append(
                (sloped * (aligned[k * ROWS : (k + 1) * ROWS] - level)).astype(BF16)
            )
        grad[b] += nn(jnp.concatenate(parts, axis=0), keys_of(c))

    def second_block(b, carry):
        def step(c, carry):
            second_pass(b, c)
            return carry

        return lax.fori_loop(0, last_chunk(b) + 1, step, carry)

    lax.fori_loop(0, 2, second_block, 0)

    wbuf[...] = jnp.zeros((LANES, WIDTH), F32)
    both = jnp.concatenate([lr[0], lr[1]], axis=1)
    for k in range(PROBES):
        stack = jnp.concatenate(
            [
                grad[b, k * ROWS : (k + 1) * ROWS] * inv[b] for b in range(2)
            ],
            axis=0,
        )
        wbuf[pl.ds(pl.multiple_of(k * 32 + head * 16, 16), RANK), :] = nn(
            both, stack, HIGHEST
        )
    turned = wbuf[...].T
    for i in range(SEQ):
        w_out[i] = turned[4 * i : 4 * i + 4]
    w_in[s] = w_out[s]
    send_seq(lambda to: w_out.at[to], w_in, 4)

    arrived(h_in, 3)
    piece = total(h_in)
    e_out[...] = piece
    e_in[s] = piece
    send_seq(lambda to: e_out, e_in, 5)

    arrived(w_in, 4)
    masked, repeated = spread(total(w_in))
    srep[KNOWN : KNOWN + PROBES] = repeated
    dots = nt(masked, srep[...], HIGHEST) * (1.0 / (RANK * 2 * tensor * WIDTH))
    c_out[...] = dots
    c_in[s] = dots
    send_seq(lambda to: c_out, c_in, 6)

    arrived(e_in, 5)
    gmat[...] = jnp.concatenate([e_in[i] for i in range(SEQ)], axis=0)
    gfull = gmat[...]
    eye = (iota((LANES, LANES), 0) == iota((LANES, LANES), 1)).astype(F32)
    square = nn(gfull, gfull, HIGHEST)
    cube = nn(square, gfull, HIGHEST)
    once = 2.0 * eye - gfull
    twice = 4.0 * (eye + square) - 6.0 * gfull - cube

    arrived(c_in, 6)
    piece = total(c_in)
    d_out[...] = piece
    d_in[t] = piece
    send_tensor(d_out, d_in, 7)
    arrived(d_in, 7)
    dots = total(d_in)

    lane = iota((PROBES, LANES), 1)
    known = jnp.where(lane < KNOWN, dots, 0.0)
    coeff = nn(known, once, HIGHEST)
    quad = nn(known, twice, HIGHEST)
    pick = (lane == iota((PROBES, LANES), 0) + NB).astype(F32)
    small = nt(jnp.concatenate([quad, pick], axis=0), known, HIGHEST)
    gram = dots[:, KNOWN : KNOWN + PROBES] - small[0:PROBES]
    out_ref[4:8] = jnp.concatenate(
        [small[PROBES:], jnp.zeros((PROBES, LANES - PROBES), F32)], axis=1
    )

    low = [[None] * PROBES for _ in range(PROBES)]
    for j in range(PROBES):
        pivot = gram[j : j + 1, j : j + 1]
        for m in range(j):
            pivot = pivot - low[j][m] * low[j][m]
        low[j][j] = jnp.sqrt(pivot)
        for i in range(j + 1, PROBES):
            entry = gram[i : i + 1, j : j + 1]
            for m in range(j):
                entry = entry - low[i][m] * low[j][m]
            low[i][j] = entry / low[j][j]
    row4, col4 = iota((PROBES, LANES), 0), iota((PROBES, LANES), 1)
    upper = jnp.zeros((PROBES, LANES), F32)
    for i in range(PROBES):
        for j in range(i + 1):
            upper = jnp.where((row4 == j) & (col4 == i), low[i][j], upper)
    out_ref[8:12] = upper

    mix = jnp.where(
        lane < KNOWN,
        -coeff,
        (lane == iota((PROBES, LANES), 0) + KNOWN).astype(F32),
    )
    residue = nn(mix, srep[...], HIGHEST)
    rows = []
    for i in range(PROBES):
        row = residue[i : i + 1]
        for m in range(i):
            row = row - low[i][m] * rows[m]
        rows.append(row / low[i][i])
    lane1 = iota((1, LANES), 1) // 32
    made = []
    for d in range(4):
        row = rows[0][:, d * LANES : (d + 1) * LANES]
        for k in range(1, PROBES):
            row = jnp.where(lane1 == k, rows[k][:, d * LANES : (d + 1) * LANES], row)
        made.append(row)
    out_ref[0:4] = jnp.concatenate(made, axis=0)

    shards = kv.at[pl.ds(0, SEQ - 1)]
    pltpu.make_async_copy(shards, shards, kv_send).wait()
    q_copy.wait_send()
    lr_copy.wait_send()
    for n, into in enumerate((lr_in, vt_in, g_in, h_in, w_in, e_in, c_in, d_in)):
        sent(into, n)


def unpack(packed, next_ref, diag_ref, sub_ref):
    for k in range(PROBES):
        for h in range(2):
            at = k * 32 + h * 16
            next_ref[k, h] = packed[0:4, at : at + 16]
    diag_ref[0] = packed[4:8, 0:PROBES]
    sub_ref[0] = packed[8:12, 0:PROBES]


def on_device(
    activations, adapter_down_weight, queries, keys, values, sequence_lengths, probe, basis
):
    tensor = lax.axis_size("tensor")
    width = activations.shape[2]
    act = activations.reshape(ROWS, width).T
    down = adapter_down_weight.T
    q = queries.reshape(2 * ROWS, WIDTH)
    k = keys.reshape(ROWS, WIDTH)
    v = values.reshape(ROWS, WIDTH)
    probe_in = probe.transpose(0, 2, 3, 1)
    basis_in = basis.transpose(1, 2, 3, 0).reshape(LANES, NB)
    anywhere = pl.BlockSpec(memory_space=pl.ANY)
    in_vmem = pl.BlockSpec(memory_space=pltpu.VMEM)
    piece = (4, LANES)
    by_seq = pltpu.VMEM((SEQ,) + piece, F32)
    by_tensor = pltpu.VMEM((tensor,) + piece, F32)
    one = pltpu.VMEM(piece, F32)
    packed = pl.pallas_call(
        functools.partial(kernel, tensor),
        out_shape=jax.ShapeDtypeStruct((16, LANES), F32),
        in_specs=[anywhere] * 5
        + [pl.BlockSpec(memory_space=pltpu.SMEM)]
        + [anywhere] * 2,
        out_specs=in_vmem,
        scratch_shapes=[
            pltpu.VMEM((width, ROWS), BF16),
            pltpu.VMEM((RANK, width), BF16),
            pltpu.VMEM((2 * ROWS, WIDTH), BF16),
            pltpu.VMEM((2 * ROWS, WIDTH), F32),
            pltpu.VMEM((3, ROWS, WIDTH), BF16),
            pltpu.VMEM((PROBES, 2, 4, RANK), F32),
            pltpu.VMEM((LANES, NB), F32),
            pltpu.VMEM((SEQ, 2, ROWS, WIDTH), BF16),
            pltpu.VMEM((2, GROUPS, (PROBES + 1) * GROUP, WIDTH), BF16),
            pltpu.VMEM((2, GROUPS, (PROBES + 2) * GROUP, 2 * WIDTH), F32),
            pltpu.VMEM((2, CHUNKS, ROWS, CHUNK), F32),
            pltpu.VMEM((2, PROBES * ROWS, WIDTH), BF16),
            pltpu.VMEM((2, PROBES * ROWS, WIDTH), F32),
            pltpu.VMEM((2, ROWS, WIDTH), F32),
            pltpu.VMEM((2, PROBES * ROWS, WIDTH), F32),
            pltpu.VMEM((LANES, WIDTH), F32),
            pltpu.VMEM((LANES, WIDTH), F32),
            pltpu.VMEM((LANES, 4 * LANES), F32),
            pltpu.VMEM((LANES, LANES), F32),
            pltpu.VMEM((RANK, ROWS), F32),
            pltpu.VMEM((tensor, RANK, ROWS), F32),
            pltpu.VMEM((2, RANK, ROWS), F32),
            one,
            by_seq,
            by_seq,
            by_seq,
            one,
            by_seq,
            one,
            by_tensor,
            by_seq,
            by_seq,
            one,
            by_tensor,
            one,
            by_seq,
            pltpu.SemaphoreType.DMA((7,)),
            pltpu.SemaphoreType.DMA,
            pltpu.SemaphoreType.DMA((4,)),
            pltpu.SemaphoreType.DMA((4, 4)),
            pltpu.SemaphoreType.DMA((4, 4)),
            pltpu.SemaphoreType.DMA((2,)),
            pltpu.SemaphoreType.DMA((2,)),
            pltpu.SemaphoreType.DMA((8,)),
            pltpu.SemaphoreType.DMA((8,)),
        ],
        compiler_params=pltpu.CompilerParams(
            collective_id=0, has_side_effects=True, vmem_limit_bytes=60 * 1024 * 1024
        ),
    )(act, down, q, k, v, sequence_lengths, probe_in, basis_in)
    turned, diag, sub = pl.pallas_call(
        unpack,
        out_shape=(
            jax.ShapeDtypeStruct((PROBES, 2, 4, RANK), F32),
            jax.ShapeDtypeStruct((1, PROBES, PROBES), F32),
            jax.ShapeDtypeStruct((1, PROBES, PROBES), F32),
        ),
        in_specs=[in_vmem],
        out_specs=(in_vmem,) * 3,
    )(packed)
    return turned.transpose(0, 3, 1, 2)[None], diag, sub


def solution(mesh):
    in_specs = (
        P(None, "seq", "tensor"),
        P("tensor", None),
        P(None, "seq", "tensor", None),
        P(None, "seq", "tensor", None),
        P(None, "seq", "tensor", None),
        P(),
        P(None, None, "tensor", "seq"),
        P(None, None, "tensor", "seq"),
    )
    out_specs = (P(None, None, None, "tensor", "seq"), P(), P())
    return jax.shard_map(
        on_device, mesh=mesh, in_specs=in_specs, out_specs=out_specs, check_vma=False
    )
```

```python
import functools

import jax
import jax.numpy as jnp
from jax import lax
from jax.experimental import pallas as pl
from jax.experimental.pallas import tpu as pltpu
from jax.sharding import PartitionSpec as P

MESH = pl.DeviceIdType.MESH
HIGHEST = lax.Precision.HIGHEST
F32 = jnp.float32
BF16 = jnp.bfloat16

adapter_scale = 0.25
query_scale = 144.0 ** (-0.5)
soft_cap = 50.0

SEQ = 32
ROWS = 128
WIDTH = 128
RANK = 16
PROBES = 4
NB = 96
KNOWN = NB + PROBES
CHUNK = 4 * ROWS
CHUNKS = SEQ // 4
GROUPS = 2
GROUP = ROWS // GROUPS
LANES = 128


def nn(a, b, precision=None):
    return lax.dot_general(
        a, b, (((1,), (0,)), ((), ())), precision=precision, preferred_element_type=F32
    )


def nt(a, b, precision=None):
    return lax.dot_general(
        a, b, (((1,), (1,)), ((), ())), precision=precision, preferred_element_type=F32
    )


def tn(a, b, precision=None):
    return lax.dot_general(
        a, b, (((0,), (0,)), ((), ())), precision=precision, preferred_element_type=F32
    )


def iota(shape, dim):
    return lax.broadcasted_iota(jnp.int32, shape, dim)


def spread(compact):
    lane = iota((PROBES, LANES), 1)
    own = (lane // 32) == iota((PROBES, LANES), 0)
    masked = [
        jnp.where(own, jnp.broadcast_to(compact[d : d + 1], (PROBES, LANES)), 0.0)
        for d in range(4)
    ]
    repeated = []
    for piece in masked:
        piece = piece + pltpu.roll(piece, 32, 1)
        repeated.append(piece + pltpu.roll(piece, 64, 1))
    return jnp.concatenate(masked, axis=1), jnp.concatenate(repeated, axis=1)


def kernel(
    tensor,
    act_hbm,
    down_hbm,
    q_hbm,
    k_hbm,
    v_hbm,
    len_ref,
    probe_hbm,
    basis_hbm,
    out_ref,
    act,
    down,
    qraw,
    qwide,
    qbuf,
    probe,
    basis,
    kv,
    lhs,
    acc,
    slopes,
    cot,
    corr,
    inv,
    grad,
    vect,
    wbuf,
    srep,
    gmat,
    lr_out,
    lr_in,
    lr,
    vt_out,
    vt_in,
    w_out,
    w_in,
    c_out,
    c_in,
    d_out,
    d_in,
    g_out,
    g_in,
    h_out,
    h_in,
    e_out,
    e_in,
    local_sem,
    kv_send,
    z_recv,
    x_recv,
    sib_recv,
    pair_send,
    pair_recv,
    ex_send,
    ex_recv,
):
    s = lax.axis_index("seq")
    t = lax.axis_index("tensor")
    x, z, core = s // 8, (s // 2) % 4, s % 2
    partner = SEQ - 1 - s
    head = s // (SEQ // 2)

    def seq_at(xx, zz, cc):
        return (lax.rem(xx + 4, 4) * 4 + lax.rem(zz + 4, 4)) * 2 + cc

    loads = [
        pltpu.make_async_copy(src, dst, local_sem.at[i])
        for i, (src, dst) in enumerate(
            (
                (act_hbm, act),
                (down_hbm, down),
                (q_hbm, qraw),
                (probe_hbm, probe),
                (basis_hbm, basis),
                (k_hbm, kv.at[s, 0]),
                (v_hbm, kv.at[s, 1]),
            )
        )
    ]
    for load in loads:
        load.start()

    barrier = pltpu.get_barrier_semaphore()

    def greet_seq(o, carry):
        pl.semaphore_signal(
            barrier, inc=1, device_id={"seq": lax.rem(s + o, SEQ)}, device_id_type=MESH
        )
        return carry

    def greet_tensor(o, carry):
        pl.semaphore_signal(
            barrier,
            inc=1,
            device_id={"tensor": lax.rem(t + o, tensor)},
            device_id_type=MESH,
        )
        return carry

    lax.fori_loop(1, SEQ, greet_seq, 0)
    lax.fori_loop(1, tensor, greet_tensor, 0)

    def send_seq(src_of, into, n):
        def body(o, carry):
            to = lax.rem(s + o, SEQ)
            pltpu.make_async_remote_copy(
                src_ref=src_of(to),
                dst_ref=into.at[s],
                send_sem=ex_send.at[n],
                recv_sem=ex_recv.at[n],
                device_id={"seq": to},
                device_id_type=MESH,
            ).start()
            return carry

        lax.fori_loop(1, SEQ, body, 0)

    def send_tensor(src, into, n):
        def body(o, carry):
            pltpu.make_async_remote_copy(
                src_ref=src,
                dst_ref=into.at[t],
                send_sem=ex_send.at[n],
                recv_sem=ex_recv.at[n],
                device_id={"tensor": lax.rem(t + o, tensor)},
                device_id_type=MESH,
            ).start()
            return carry

        lax.fori_loop(1, tensor, body, 0)

    def arrived(into, n):
        span = into.at[pl.ds(0, into.shape[0] - 1)]
        pltpu.make_async_copy(span, span, ex_recv.at[n]).wait()

    def sent(into, n):
        span = into.at[pl.ds(0, into.shape[0] - 1)]
        pltpu.make_async_copy(span, span, ex_send.at[n]).wait()

    def total(into):
        terms = [into[i] for i in range(into.shape[0])]
        while len(terms) > 1:
            terms = [u + v for u, v in zip(terms[::2], terms[1::2])]
        return terms[0]

    def push(src, to, sem):
        pltpu.make_async_remote_copy(
            src_ref=src,
            dst_ref=src,
            send_sem=kv_send,
            recv_sem=sem,
            device_id={"seq": to},
            device_id_type=MESH,
        ).start()

    def came(ref, sem):
        pltpu.make_async_copy(ref, ref, sem).wait()

    z_up, z_down = seq_at(x, z + 1, core), seq_at(x, z + 3, core)
    x_up, x_down = seq_at(x + 1, z, core), seq_at(x + 3, z, core)
    sibling = seq_at(x, z, 1 - core)

    def push_column(d, j):
        src = kv.at[seq_at(x, z + d, core), j]
        if j == 0:
            push(src, x_up, x_recv.at[d, 0])
            push(src, x_down, x_recv.at[d, 2])
        else:
            push(src, x_down, x_recv.at[d, 3])
            push(src, x_up, x_recv.at[d, 1])
        push(src, sibling, sib_recv.at[0, d, j])

    def take_below(d, j):
        half = kv.at[seq_at(x + 3, z + d, core), j]
        came(half, x_recv.at[d, j])
        if j == 0:
            push(half, x_up, x_recv.at[d, 4])
        push(half, sibling, sib_recv.at[3, d, j])

    def take_above(d, j):
        half = kv.at[seq_at(x + 1, z + d, core), j]
        came(half, x_recv.at[d, 2 + j])
        if j == 1:
            push(half, x_down, x_recv.at[d, 5])
        push(half, sibling, sib_recv.at[1, d, j])

    def pass_x(d):
        take_below(d, 0)
        take_above(d, 1)
        take_below(d, 1)
        take_above(d, 0)

    def pass_far(d):
        for j in range(2):
            half = kv.at[seq_at(x + 2, z + d, core), j]
            came(half, x_recv.at[d, 4 + j])
            push(half, sibling, sib_recv.at[2, d, j])

    loads[0].wait()
    loads[1].wait()
    partial = nn(down[...], act[...])
    lr_out[...] = partial
    lr_in[t] = partial

    loads[3].wait()
    compact = jnp.concatenate(
        [probe[k, h] for k in range(PROBES) for h in range(2)], axis=1
    )
    vt_out[...] = compact
    vt_in[s] = compact

    loads[2].wait()
    qwide[...] = qraw[...].astype(F32)
    qbuf[0] = qwide[pl.ds(head, ROWS, stride=2), :].astype(BF16)
    qbuf[2] = qwide[pl.ds(1 - head, ROWS, stride=2), :].astype(BF16)

    loads[4].wait()
    inner = iota((LANES, 4 * LANES), 0)
    outer = iota((LANES, 4 * LANES), 1)
    place = (
        (inner // 8 == outer % 16)
        & ((inner // 4) % 2 == (outer // 16) % 2)
        & (inner % 4 == outer // LANES)
    )
    srep[...] = jnp.zeros((LANES, 4 * LANES), F32)
    srep[0:NB] = tn(basis[...], place.astype(F32), HIGHEST)
    srep[NB:KNOWN] = spread(compact)[1]
    kinds = srep[...]
    gram = nt(kinds, kinds, HIGHEST) * (0.25 / (RANK * 2 * tensor * WIDTH))
    for i in range(SEQ):
        g_out[i] = gram[4 * i : 4 * i + 4]
    g_in[s] = g_out[s]
    loads[5].wait()
    loads[6].wait()

    pl.semaphore_wait(barrier, SEQ - 1 + tensor - 1)
    push(kv.at[s, 0], z_up, z_recv.at[0])
    push(kv.at[s, 1], z_down, z_recv.at[3])
    push(kv.at[s, 1], z_up, z_recv.at[1])
    push(kv.at[s, 0], z_down, z_recv.at[2])
    push_column(0, 0)
    push_column(0, 1)
    send_tensor(lr_out, lr_in, 0)
    send_seq(lambda to: vt_out, vt_in, 1)
    q_copy = pltpu.make_async_remote_copy(
        src_ref=qbuf.at[2],
        dst_ref=qbuf.at[1],
        send_sem=pair_send.at[0],
        recv_sem=pair_recv.at[0],
        device_id={"seq": partner},
        device_id_type=MESH,
    )
    q_copy.start()

    below = seq_at(x, z + 3, core)
    above = seq_at(x, z + 1, core)
    take_below(0, 0)
    take_above(0, 1)
    came(kv.at[below, 0], z_recv.at[0])
    push(kv.at[below, 0], z_up, z_recv.at[4])
    push_column(3, 0)
    came(kv.at[above, 1], z_recv.at[3])
    push(kv.at[above, 1], z_down, z_recv.at[5])
    push_column(1, 1)
    came(kv.at[below, 1], z_recv.at[1])
    push_column(3, 1)
    came(kv.at[above, 0], z_recv.at[2])
    push_column(1, 0)
    take_below(0, 1)
    take_above(0, 0)

    arrived(lr_in, 0)
    lr[0] = total(lr_in)
    lr_copy = pltpu.make_async_remote_copy(
        src_ref=lr.at[0],
        dst_ref=lr.at[1],
        send_sem=pair_send.at[1],
        recv_sem=pair_recv.at[1],
        device_id={"seq": partner},
        device_id_type=MESH,
    )
    lr_copy.start()

    far = seq_at(x, z + 2, core)
    came(kv.at[far, 0], z_recv.at[4])
    push_column(2, 0)
    came(kv.at[far, 1], z_recv.at[5])
    push_column(2, 1)
    pass_far(0)
    pass_x(3)
    pass_x(1)

    arrived(vt_in, 1)
    vect[...] = jnp.concatenate([vt_in[i] for i in range(SEQ)], axis=0).T

    def left_side(b):
        low = lr[b]
        query = qbuf[b]
        for g in range(GROUPS):
            lhs[b, g, 0:GROUP] = query[g * GROUP : (g + 1) * GROUP]
        for k in range(PROBES):
            vk = vect[pl.ds(pl.multiple_of(k * 32 + head * 16, 16), RANK), :]
            tangent = (adapter_scale * tn(low, vk, HIGHEST)).astype(BF16)
            for g in range(GROUPS):
                lhs[b, g, (k + 1) * GROUP : (k + 2) * GROUP] = tangent[
                    g * GROUP : (g + 1) * GROUP
                ]

    left_side(0)
    send_seq(lambda to: g_out.at[to], g_in, 2)
    q_copy.wait_recv()
    lr_copy.wait_recv()
    left_side(1)

    acc[...] = jnp.zeros(acc.shape, F32)
    ones = jnp.ones((CHUNK, WIDTH), BF16)
    length = len_ref[0]

    def first_of(b):
        return jnp.where(b == 0, s, partner) * ROWS

    def last_chunk(b):
        return jnp.where(b == 0, s, partner) // 4

    def keys_of(c):
        return jnp.concatenate([kv[4 * c + i, 0] for i in range(4)], axis=0)

    def values_of(c):
        return jnp.concatenate([kv[4 * c + i, 1] for i in range(4)], axis=0)

    def first_pass(b, c):
        keys = keys_of(c)
        ext = jnp.concatenate([values_of(c), ones], axis=1)
        for g in range(GROUPS):
            scores = nt(lhs[b, g], keys)
            capped = jnp.tanh(scores[0:GROUP] * (query_scale / soft_cap))
            row = first_of(b) + g * GROUP + iota((GROUP, 1), 0)
            limit = jnp.minimum(row, length - 1) - c * CHUNK
            weights = jnp.where(
                iota((GROUP, CHUNK), 1) <= limit, jnp.exp(soft_cap * capped), 0.0
            )
            sloped = weights * (1.0 - capped * capped)
            slopes[b, c, g * GROUP : (g + 1) * GROUP] = sloped
            high = weights.astype(BF16)
            parts = [high, (weights - high.astype(F32)).astype(BF16)]
            for k in range(PROBES):
                parts.append(
                    (sloped * scores[(k + 1) * GROUP : (k + 2) * GROUP]).astype(BF16)
                )
            acc[b, g] += nn(jnp.concatenate(parts, axis=0), ext)

    def column_step(q, carry):
        e = jnp.where(q == 0, 0, jnp.where(q == 1, 3, q - 1))

        @pl.when(q == 1)
        def _():
            pass_x(2)
            pass_far(3)
            pass_far(1)

        @pl.when(q == 3)
        def _():
            pass_far(2)

        def pair_step(p, carry):
            pair = lax.rem(z // 2 + p, 2)
            for i in range(2):
                other = seq_at(x + e, 2 * pair + i, 1 - core)
                d = lax.rem(2 * pair + i - z + 4, 4)
                came(kv.at[other, 0], sib_recv.at[e, d, 0])
                came(kv.at[other, 1], sib_recv.at[e, d, 1])
            c = seq_at(x + e, 2 * pair, 0) // 4

            def block_step(b, carry):
                @pl.when(c <= last_chunk(b))
                def _():
                    first_pass(b, c)

                return carry

            return lax.fori_loop(0, 2, block_step, carry)

        return lax.fori_loop(0, 2, pair_step, carry)

    lax.fori_loop(0, 4, column_step, 0)

    arrived(g_in, 2)
    piece = total(g_in)
    h_out[...] = piece
    h_in[t] = piece
    send_tensor(h_out, h_in, 3)

    def turn(b, carry):
        for g in range(GROUPS):
            full = acc[b, g]
            plain = full[0:GROUP] + full[GROUP : 2 * GROUP]
            share = 1.0 / plain[:, WIDTH:]
            attended = plain[:, :WIDTH] * share
            share_scaled = share * query_scale
            row = first_of(b) + g * GROUP + iota((GROUP, 1), 0)
            valid = row < length
            for k in range(PROBES):
                part = full[(k + 2) * GROUP : (k + 3) * GROUP]
                tangent = (part[:, :WIDTH] - part[:, WIDTH:] * attended) * share_scaled
                tangent = jnp.where(valid, tangent, 0.0)
                at = k * ROWS + g * GROUP
                cot[b, at : at + GROUP] = tangent.astype(BF16)
                corr[b, at : at + GROUP] = jnp.broadcast_to(
                    jnp.sum(tangent * attended, axis=1, keepdims=True), (GROUP, WIDTH)
                )
            inv[b, g * GROUP : (g + 1) * GROUP] = share * (
                query_scale * adapter_scale / (SEQ * ROWS)
            )
        return carry

    lax.fori_loop(0, 2, turn, 0)

    grad[...] = jnp.zeros(grad.shape, F32)

    def two(part, c):
        return jnp.concatenate([part(2 * c), part(2 * c + 1)], axis=0)

    def second_pass(b, c):
        aligned = nt(cot[b], two(values_of, c))
        sloped = jnp.concatenate([slopes[b, 2 * c], slopes[b, 2 * c + 1]], axis=1)
        parts = []
        for k in range(PROBES):
            level = corr[b, k * ROWS : (k + 1) * ROWS]
            level = jnp.concatenate([level] * (2 * CHUNK // WIDTH), axis=1)
            parts.append(
                (sloped * (aligned[k * ROWS : (k + 1) * ROWS] - level)).astype(BF16)
            )
        grad[b] += nn(jnp.concatenate(parts, axis=0), two(keys_of, c))

    def second_block(b, carry):
        def step(c, carry):
            second_pass(b, c)
            return carry

        last = last_chunk(b)

        @pl.when(last % 2 == 0)
        def _():
            slopes[b, last + 1] = jnp.zeros((ROWS, CHUNK), F32)

        return lax.fori_loop(0, last // 2 + 1, step, carry)

    lax.fori_loop(0, 2, second_block, 0)

    wbuf[...] = jnp.zeros((LANES, WIDTH), F32)
    both = jnp.concatenate([lr[0], lr[1]], axis=1)
    for k in range(PROBES):
        stack = jnp.concatenate(
            [
                grad[b, k * ROWS : (k + 1) * ROWS] * inv[b] for b in range(2)
            ],
            axis=0,
        )
        wbuf[pl.ds(pl.multiple_of(k * 32 + head * 16, 16), RANK), :] = nn(
            both, stack, HIGHEST
        )
    turned = wbuf[...].T
    for i in range(SEQ):
        w_out[i] = turned[4 * i : 4 * i + 4]
    w_in[s] = w_out[s]
    send_seq(lambda to: w_out.at[to], w_in, 4)

    arrived(h_in, 3)
    piece = total(h_in)
    e_out[...] = piece
    e_in[s] = piece
    send_seq(lambda to: e_out, e_in, 5)

    arrived(w_in, 4)
    masked, repeated = spread(total(w_in))
    srep[KNOWN : KNOWN + PROBES] = repeated
    dots = nt(masked, srep[...], HIGHEST) * (1.0 / (RANK * 2 * tensor * WIDTH))
    c_out[...] = dots
    c_in[s] = dots
    send_seq(lambda to: c_out, c_in, 6)

    arrived(e_in, 5)
    gmat[...] = jnp.concatenate([e_in[i] for i in range(SEQ)], axis=0)
    gfull = gmat[...]
    eye = (iota((LANES, LANES), 0) == iota((LANES, LANES), 1)).astype(F32)
    square = nn(gfull, gfull, HIGHEST)
    cube = nn(square, gfull, HIGHEST)
    once = 2.0 * eye - gfull
    twice = 4.0 * (eye + square) - 6.0 * gfull - cube

    arrived(c_in, 6)
    piece = total(c_in)
    d_out[...] = piece
    d_in[t] = piece
    send_tensor(d_out, d_in, 7)
    arrived(d_in, 7)
    dots = total(d_in)

    lane = iota((PROBES, LANES), 1)
    known = jnp.where(lane < KNOWN, dots, 0.0)
    coeff = nn(known, once, HIGHEST)
    quad = nn(known, twice, HIGHEST)
    pick = (lane == iota((PROBES, LANES), 0) + NB).astype(F32)
    small = nt(jnp.concatenate([quad, pick], axis=0), known, HIGHEST)
    gram = dots[:, KNOWN : KNOWN + PROBES] - small[0:PROBES]
    out_ref[4:8] = jnp.concatenate(
        [small[PROBES:], jnp.zeros((PROBES, LANES - PROBES), F32)], axis=1
    )

    low = [[None] * PROBES for _ in range(PROBES)]
    for j in range(PROBES):
        pivot = gram[j : j + 1, j : j + 1]
        for m in range(j):
            pivot = pivot - low[j][m] * low[j][m]
        low[j][j] = jnp.sqrt(pivot)
        for i in range(j + 1, PROBES):
            entry = gram[i : i + 1, j : j + 1]
            for m in range(j):
                entry = entry - low[i][m] * low[j][m]
            low[i][j] = entry / low[j][j]
    row4, col4 = iota((PROBES, LANES), 0), iota((PROBES, LANES), 1)
    upper = jnp.zeros((PROBES, LANES), F32)
    for i in range(PROBES):
        for j in range(i + 1):
            upper = jnp.where((row4 == j) & (col4 == i), low[i][j], upper)
    out_ref[8:12] = upper

    mix = jnp.where(
        lane < KNOWN,
        -coeff,
        (lane == iota((PROBES, LANES), 0) + KNOWN).astype(F32),
    )
    residue = nn(mix, srep[...], HIGHEST)
    rows = []
    for i in range(PROBES):
        row = residue[i : i + 1]
        for m in range(i):
            row = row - low[i][m] * rows[m]
        rows.append(row / low[i][i])
    lane1 = iota((1, LANES), 1) // 32
    made = []
    for d in range(4):
        row = rows[0][:, d * LANES : (d + 1) * LANES]
        for k in range(1, PROBES):
            row = jnp.where(lane1 == k, rows[k][:, d * LANES : (d + 1) * LANES], row)
        made.append(row)
    out_ref[0:4] = jnp.concatenate(made, axis=0)

    shards = kv.at[pl.ds(0, SEQ - 1)]
    pltpu.make_async_copy(shards, shards, kv_send).wait()
    q_copy.wait_send()
    lr_copy.wait_send()
    for n, into in enumerate((lr_in, vt_in, g_in, h_in, w_in, e_in, c_in, d_in)):
        sent(into, n)


def unpack(packed, next_ref, diag_ref, sub_ref):
    for k in range(PROBES):
        for h in range(2):
            at = k * 32 + h * 16
            next_ref[k, h] = packed[0:4, at : at + 16]
    diag_ref[0] = packed[4:8, 0:PROBES]
    sub_ref[0] = packed[8:12, 0:PROBES]


def on_device(
    activations, adapter_down_weight, queries, keys, values, sequence_lengths, probe, basis
):
    tensor = lax.axis_size("tensor")
    width = activations.shape[2]
    act = activations.reshape(ROWS, width).T
    down = adapter_down_weight.T
    q = queries.reshape(2 * ROWS, WIDTH)
    k = keys.reshape(ROWS, WIDTH)
    v = values.reshape(ROWS, WIDTH)
    probe_in = probe.transpose(0, 2, 3, 1)
    basis_in = basis.transpose(1, 2, 3, 0).reshape(LANES, NB)
    anywhere = pl.BlockSpec(memory_space=pl.ANY)
    in_vmem = pl.BlockSpec(memory_space=pltpu.VMEM)
    piece = (4, LANES)
    by_seq = pltpu.VMEM((SEQ,) + piece, F32)
    by_tensor = pltpu.VMEM((tensor,) + piece, F32)
    one = pltpu.VMEM(piece, F32)
    packed = pl.pallas_call(
        functools.partial(kernel, tensor),
        out_shape=jax.ShapeDtypeStruct((16, LANES), F32),
        in_specs=[anywhere] * 5
        + [pl.BlockSpec(memory_space=pltpu.SMEM)]
        + [anywhere] * 2,
        out_specs=in_vmem,
        scratch_shapes=[
            pltpu.VMEM((width, ROWS), BF16),
            pltpu.VMEM((RANK, width), BF16),
            pltpu.VMEM((2 * ROWS, WIDTH), BF16),
            pltpu.VMEM((2 * ROWS, WIDTH), F32),
            pltpu.VMEM((3, ROWS, WIDTH), BF16),
            pltpu.VMEM((PROBES, 2, 4, RANK), F32),
            pltpu.VMEM((LANES, NB), F32),
            pltpu.VMEM((SEQ, 2, ROWS, WIDTH), BF16),
            pltpu.VMEM((2, GROUPS, (PROBES + 1) * GROUP, WIDTH), BF16),
            pltpu.VMEM((2, GROUPS, (PROBES + 2) * GROUP, 2 * WIDTH), F32),
            pltpu.VMEM((2, CHUNKS, ROWS, CHUNK), F32),
            pltpu.VMEM((2, PROBES * ROWS, WIDTH), BF16),
            pltpu.VMEM((2, PROBES * ROWS, WIDTH), F32),
            pltpu.VMEM((2, ROWS, WIDTH), F32),
            pltpu.VMEM((2, PROBES * ROWS, WIDTH), F32),
            pltpu.VMEM((LANES, WIDTH), F32),
            pltpu.VMEM((LANES, WIDTH), F32),
            pltpu.VMEM((LANES, 4 * LANES), F32),
            pltpu.VMEM((LANES, LANES), F32),
            pltpu.VMEM((RANK, ROWS), F32),
            pltpu.VMEM((tensor, RANK, ROWS), F32),
            pltpu.VMEM((2, RANK, ROWS), F32),
            one,
            by_seq,
            by_seq,
            by_seq,
            one,
            by_seq,
            one,
            by_tensor,
            by_seq,
            by_seq,
            one,
            by_tensor,
            one,
            by_seq,
            pltpu.SemaphoreType.DMA((7,)),
            pltpu.SemaphoreType.DMA,
            pltpu.SemaphoreType.DMA((6,)),
            pltpu.SemaphoreType.DMA((4, 6)),
            pltpu.SemaphoreType.DMA((4, 4, 2)),
            pltpu.SemaphoreType.DMA((2,)),
            pltpu.SemaphoreType.DMA((2,)),
            pltpu.SemaphoreType.DMA((8,)),
            pltpu.SemaphoreType.DMA((8,)),
        ],
        compiler_params=pltpu.CompilerParams(
            collective_id=0, has_side_effects=True, vmem_limit_bytes=60 * 1024 * 1024
        ),
    )(act, down, q, k, v, sequence_lengths, probe_in, basis_in)
    turned, diag, sub = pl.pallas_call(
        unpack,
        out_shape=(
            jax.ShapeDtypeStruct((PROBES, 2, 4, RANK), F32),
            jax.ShapeDtypeStruct((1, PROBES, PROBES), F32),
            jax.ShapeDtypeStruct((1, PROBES, PROBES), F32),
        ),
        in_specs=[in_vmem],
        out_specs=(in_vmem,) * 3,
    )(packed)
    return turned.transpose(0, 3, 1, 2)[None], diag, sub


def solution(mesh):
    in_specs = (
        P(None, "seq", "tensor"),
        P("tensor", None),
        P(None, "seq", "tensor", None),
        P(None, "seq", "tensor", None),
        P(None, "seq", "tensor", None),
        P(),
        P(None, None, "tensor", "seq"),
        P(None, None, "tensor", "seq"),
    )
    out_specs = (P(None, None, None, "tensor", "seq"), P(), P())
    return jax.shard_map(
        on_device, mesh=mesh, in_specs=in_specs, out_specs=out_specs, check_vma=False
    )
```

```python
import functools

import jax
import jax.numpy as jnp
from jax import lax
from jax.experimental import pallas as pl
from jax.experimental.pallas import tpu as pltpu
from jax.sharding import PartitionSpec as P

MESH = pl.DeviceIdType.MESH
HIGHEST = lax.Precision.HIGHEST
F32 = jnp.float32
BF16 = jnp.bfloat16

adapter_scale = 0.25
query_scale = 144.0 ** (-0.5)
soft_cap = 50.0

SEQ = 32
ROWS = 128
WIDTH = 128
RANK = 16
PROBES = 4
NB = 96
KNOWN = NB + PROBES
CHUNK = 4 * ROWS
CHUNKS = SEQ // 4
GROUPS = 2
GROUP = ROWS // GROUPS
LANES = 128


def nn(a, b, precision=None):
    return lax.dot_general(
        a, b, (((1,), (0,)), ((), ())), precision=precision, preferred_element_type=F32
    )


def nt(a, b, precision=None):
    return lax.dot_general(
        a, b, (((1,), (1,)), ((), ())), precision=precision, preferred_element_type=F32
    )


def tn(a, b, precision=None):
    return lax.dot_general(
        a, b, (((0,), (0,)), ((), ())), precision=precision, preferred_element_type=F32
    )


def iota(shape, dim):
    return lax.broadcasted_iota(jnp.int32, shape, dim)


def spread(compact):
    lane = iota((PROBES, LANES), 1)
    own = (lane // 32) == iota((PROBES, LANES), 0)
    masked = [
        jnp.where(own, jnp.broadcast_to(compact[d : d + 1], (PROBES, LANES)), 0.0)
        for d in range(4)
    ]
    repeated = []
    for piece in masked:
        piece = piece + pltpu.roll(piece, 32, 1)
        repeated.append(piece + pltpu.roll(piece, 64, 1))
    return jnp.concatenate(masked, axis=1), jnp.concatenate(repeated, axis=1)


def kernel(
    tensor,
    act_hbm,
    down_hbm,
    q_hbm,
    k_hbm,
    v_hbm,
    len_ref,
    probe_hbm,
    basis_hbm,
    out_ref,
    act,
    down,
    qraw,
    qwide,
    qbuf,
    probe,
    basis,
    kv,
    lhs,
    acc,
    slopes,
    cot,
    corr,
    inv,
    grad,
    vect,
    wbuf,
    srep,
    gmat,
    lr_out,
    lr_in,
    lr,
    vt_out,
    vt_in,
    w_out,
    w_in,
    c_out,
    c_in,
    d_out,
    d_in,
    g_out,
    g_in,
    h_out,
    h_in,
    e_out,
    e_in,
    local_sem,
    kv_send,
    z_recv,
    x_recv,
    sib_recv,
    pair_send,
    pair_recv,
    ex_send,
    ex_recv,
):
    s = lax.axis_index("seq")
    t = lax.axis_index("tensor")
    x, z, core = s // 8, (s // 2) % 4, s % 2
    partner = SEQ - 1 - s
    head = s // (SEQ // 2)

    def seq_at(xx, zz, cc):
        return (lax.rem(xx + 4, 4) * 4 + lax.rem(zz + 4, 4)) * 2 + cc

    loads = [
        pltpu.make_async_copy(src, dst, local_sem.at[i])
        for i, (src, dst) in enumerate(
            (
                (act_hbm, act),
                (down_hbm, down),
                (q_hbm, qraw),
                (probe_hbm, probe),
                (basis_hbm, basis),
                (k_hbm, kv.at[s, 0]),
                (v_hbm, kv.at[s, 1]),
            )
        )
    ]
    for load in loads:
        load.start()

    barrier = pltpu.get_barrier_semaphore()

    def greet_seq(o, carry):
        pl.semaphore_signal(
            barrier, inc=1, device_id={"seq": lax.rem(s + o, SEQ)}, device_id_type=MESH
        )
        return carry

    def greet_tensor(o, carry):
        pl.semaphore_signal(
            barrier,
            inc=1,
            device_id={"tensor": lax.rem(t + o, tensor)},
            device_id_type=MESH,
        )
        return carry

    lax.fori_loop(1, SEQ, greet_seq, 0)
    lax.fori_loop(1, tensor, greet_tensor, 0)

    def send_seq(src_of, into, n):
        def body(o, carry):
            to = lax.rem(s + 1 + lax.rem(o + 14, SEQ - 1), SEQ)
            pltpu.make_async_remote_copy(
                src_ref=src_of(to),
                dst_ref=into.at[s],
                send_sem=ex_send.at[n],
                recv_sem=ex_recv.at[n],
                device_id={"seq": to},
                device_id_type=MESH,
            ).start()
            return carry

        lax.fori_loop(1, SEQ, body, 0)

    def send_tensor(src, into, n):
        def body(o, carry):
            pltpu.make_async_remote_copy(
                src_ref=src,
                dst_ref=into.at[t],
                send_sem=ex_send.at[n],
                recv_sem=ex_recv.at[n],
                device_id={"tensor": lax.rem(t + o, tensor)},
                device_id_type=MESH,
            ).start()
            return carry

        lax.fori_loop(1, tensor, body, 0)

    def arrived(into, n):
        span = into.at[pl.ds(0, into.shape[0] - 1)]
        pltpu.make_async_copy(span, span, ex_recv.at[n]).wait()

    def sent(into, n):
        span = into.at[pl.ds(0, into.shape[0] - 1)]
        pltpu.make_async_copy(span, span, ex_send.at[n]).wait()

    def total(into):
        terms = [into[i] for i in range(into.shape[0])]
        while len(terms) > 1:
            terms = [u + v for u, v in zip(terms[::2], terms[1::2])]
        return terms[0]

    def push(src, to, sem):
        pltpu.make_async_remote_copy(
            src_ref=src,
            dst_ref=src,
            send_sem=kv_send,
            recv_sem=sem,
            device_id={"seq": to},
            device_id_type=MESH,
        ).start()

    def came(ref, sem):
        pltpu.make_async_copy(ref, ref, sem).wait()

    z_up, z_down = seq_at(x, z + 1, core), seq_at(x, z + 3, core)
    x_up, x_down = seq_at(x + 1, z, core), seq_at(x + 3, z, core)
    sibling = seq_at(x, z, 1 - core)

    def push_column(d, j):
        src = kv.at[seq_at(x, z + d, core), j]
        if j == 0:
            push(src, x_up, x_recv.at[d, 0])
            push(src, x_down, x_recv.at[d, 2])
        else:
            push(src, x_down, x_recv.at[d, 3])
            push(src, x_up, x_recv.at[d, 1])
        push(src, sibling, sib_recv.at[0, d, j])

    def take_below(d, j):
        half = kv.at[seq_at(x + 3, z + d, core), j]
        came(half, x_recv.at[d, j])
        if j == 0:
            push(half, x_up, x_recv.at[d, 4])
        push(half, sibling, sib_recv.at[3, d, j])

    def take_above(d, j):
        half = kv.at[seq_at(x + 1, z + d, core), j]
        came(half, x_recv.at[d, 2 + j])
        if j == 1:
            push(half, x_down, x_recv.at[d, 5])
        push(half, sibling, sib_recv.at[1, d, j])

    def pass_x(d):
        take_below(d, 0)
        take_above(d, 1)
        take_below(d, 1)
        take_above(d, 0)

    def pass_far(d):
        for j in range(2):
            half = kv.at[seq_at(x + 2, z + d, core), j]
            came(half, x_recv.at[d, 4 + j])
            push(half, sibling, sib_recv.at[2, d, j])

    loads[0].wait()
    loads[1].wait()
    partial = nn(down[...], act[...])
    lr_out[...] = partial
    lr_in[t] = partial

    loads[3].wait()
    compact = jnp.concatenate(
        [probe[k, h] for k in range(PROBES) for h in range(2)], axis=1
    )
    vt_out[...] = compact
    vt_in[s] = compact

    loads[2].wait()
    qwide[...] = qraw[...].astype(F32)
    qbuf[0] = qwide[pl.ds(head, ROWS, stride=2), :].astype(BF16)
    qbuf[2] = qwide[pl.ds(1 - head, ROWS, stride=2), :].astype(BF16)

    loads[4].wait()
    inner = iota((LANES, 4 * LANES), 0)
    outer = iota((LANES, 4 * LANES), 1)
    place = (
        (inner // 8 == outer % 16)
        & ((inner // 4) % 2 == (outer // 16) % 2)
        & (inner % 4 == outer // LANES)
    )
    srep[...] = jnp.zeros((LANES, 4 * LANES), F32)
    srep[0:NB] = tn(basis[...], place.astype(F32), HIGHEST)
    srep[NB:KNOWN] = spread(compact)[1]
    kinds = srep[...]
    gram = nt(kinds, kinds, HIGHEST) * (0.25 / (RANK * 2 * tensor * WIDTH))
    for i in range(SEQ):
        g_out[i] = gram[4 * i : 4 * i + 4]
    g_in[s] = g_out[s]
    loads[5].wait()
    loads[6].wait()

    pl.semaphore_wait(barrier, SEQ - 1 + tensor - 1)
    push(kv.at[s, 0], z_up, z_recv.at[0])
    push(kv.at[s, 1], z_down, z_recv.at[3])
    push(kv.at[s, 1], z_up, z_recv.at[1])
    push(kv.at[s, 0], z_down, z_recv.at[2])
    push_column(0, 0)
    push_column(0, 1)
    send_tensor(lr_out, lr_in, 0)
    send_seq(lambda to: vt_out, vt_in, 1)
    q_copy = pltpu.make_async_remote_copy(
        src_ref=qbuf.at[2],
        dst_ref=qbuf.at[1],
        send_sem=pair_send.at[0],
        recv_sem=pair_recv.at[0],
        device_id={"seq": partner},
        device_id_type=MESH,
    )
    q_copy.start()

    below = seq_at(x, z + 3, core)
    above = seq_at(x, z + 1, core)
    take_below(0, 0)
    take_above(0, 1)
    came(kv.at[below, 0], z_recv.at[0])
    push(kv.at[below, 0], z_up, z_recv.at[4])
    push_column(3, 0)
    came(kv.at[above, 1], z_recv.at[3])
    push(kv.at[above, 1], z_down, z_recv.at[5])
    push_column(1, 1)
    came(kv.at[below, 1], z_recv.at[1])
    push_column(3, 1)
    came(kv.at[above, 0], z_recv.at[2])
    push_column(1, 0)
    take_below(0, 1)
    take_above(0, 0)

    arrived(lr_in, 0)
    lr[0] = total(lr_in)
    lr_copy = pltpu.make_async_remote_copy(
        src_ref=lr.at[0],
        dst_ref=lr.at[1],
        send_sem=pair_send.at[1],
        recv_sem=pair_recv.at[1],
        device_id={"seq": partner},
        device_id_type=MESH,
    )
    lr_copy.start()

    far = seq_at(x, z + 2, core)
    came(kv.at[far, 0], z_recv.at[4])
    push_column(2, 0)
    came(kv.at[far, 1], z_recv.at[5])
    push_column(2, 1)
    pass_far(0)
    pass_x(3)
    pass_x(1)

    arrived(vt_in, 1)
    vect[...] = jnp.concatenate([vt_in[i] for i in range(SEQ)], axis=0).T

    def left_side(b):
        low = lr[b]
        query = qbuf[b]
        for g in range(GROUPS):
            lhs[b, g, 0:GROUP] = query[g * GROUP : (g + 1) * GROUP]
        for k in range(PROBES):
            vk = vect[pl.ds(pl.multiple_of(k * 32 + head * 16, 16), RANK), :]
            tangent = (adapter_scale * tn(low, vk, HIGHEST)).astype(BF16)
            for g in range(GROUPS):
                lhs[b, g, (k + 1) * GROUP : (k + 2) * GROUP] = tangent[
                    g * GROUP : (g + 1) * GROUP
                ]

    left_side(0)
    send_seq(lambda to: g_out.at[to], g_in, 2)
    q_copy.wait_recv()
    lr_copy.wait_recv()
    left_side(1)

    acc[...] = jnp.zeros(acc.shape, F32)
    ones = jnp.ones((CHUNK, WIDTH), BF16)
    length = len_ref[0]

    def first_of(b):
        return jnp.where(b == 0, s, partner) * ROWS

    def last_chunk(b):
        return jnp.where(b == 0, s, partner) // 4

    def keys_of(c):
        return jnp.concatenate([kv[4 * c + i, 0] for i in range(4)], axis=0)

    def values_of(c):
        return jnp.concatenate([kv[4 * c + i, 1] for i in range(4)], axis=0)

    def first_pass(b, c):
        keys = keys_of(c)
        ext = jnp.concatenate([values_of(c), ones], axis=1)
        for g in range(GROUPS):
            scores = nt(lhs[b, g], keys)
            capped = jnp.tanh(scores[0:GROUP] * (query_scale / soft_cap))
            row = first_of(b) + g * GROUP + iota((GROUP, 1), 0)
            limit = jnp.minimum(row, length - 1) - c * CHUNK
            weights = jnp.where(
                iota((GROUP, CHUNK), 1) <= limit, jnp.exp(soft_cap * capped), 0.0
            )
            sloped = weights * (1.0 - capped * capped)
            slopes[b, c, g * GROUP : (g + 1) * GROUP] = sloped
            high = weights.astype(BF16)
            parts = [high, (weights - high.astype(F32)).astype(BF16)]
            for k in range(PROBES):
                parts.append(
                    (sloped * scores[(k + 1) * GROUP : (k + 2) * GROUP]).astype(BF16)
                )
            acc[b, g] += nn(jnp.concatenate(parts, axis=0), ext)

    def column_step(q, carry):
        e = jnp.where(q == 0, 0, jnp.where(q == 1, 3, q - 1))

        @pl.when(q == 1)
        def _():
            pass_x(2)
            pass_far(3)
            pass_far(1)

        @pl.when(q == 3)
        def _():
            pass_far(2)

        def pair_step(p, carry):
            pair = lax.rem(z // 2 + p, 2)
            for i in range(2):
                other = seq_at(x + e, 2 * pair + i, 1 - core)
                d = lax.rem(2 * pair + i - z + 4, 4)
                came(kv.at[other, 0], sib_recv.at[e, d, 0])
                came(kv.at[other, 1], sib_recv.at[e, d, 1])
            c = seq_at(x + e, 2 * pair, 0) // 4

            def block_step(b, carry):
                @pl.when(c <= last_chunk(b))
                def _():
                    first_pass(b, c)

                return carry

            return lax.fori_loop(0, 2, block_step, carry)

        return lax.fori_loop(0, 2, pair_step, carry)

    lax.fori_loop(0, 4, column_step, 0)

    arrived(g_in, 2)
    piece = total(g_in)
    h_out[...] = piece
    h_in[t] = piece
    send_tensor(h_out, h_in, 3)

    def turn(b, carry):
        for g in range(GROUPS):
            full = acc[b, g]
            plain = full[0:GROUP] + full[GROUP : 2 * GROUP]
            share = 1.0 / plain[:, WIDTH:]
            attended = plain[:, :WIDTH] * share
            share_scaled = share * query_scale
            row = first_of(b) + g * GROUP + iota((GROUP, 1), 0)
            valid = row < length
            for k in range(PROBES):
                part = full[(k + 2) * GROUP : (k + 3) * GROUP]
                tangent = (part[:, :WIDTH] - part[:, WIDTH:] * attended) * share_scaled
                tangent = jnp.where(valid, tangent, 0.0)
                at = k * ROWS + g * GROUP
                cot[b, at : at + GROUP] = tangent.astype(BF16)
                corr[b, at : at + GROUP] = jnp.broadcast_to(
                    jnp.sum(tangent * attended, axis=1, keepdims=True), (GROUP, WIDTH)
                )
            inv[b, g * GROUP : (g + 1) * GROUP] = share * (
                query_scale * adapter_scale / (SEQ * ROWS)
            )
        return carry

    lax.fori_loop(0, 2, turn, 0)

    grad[...] = jnp.zeros(grad.shape, F32)

    def two(part, c):
        return jnp.concatenate([part(2 * c), part(2 * c + 1)], axis=0)

    def second_pass(b, c):
        aligned = nt(cot[b], two(values_of, c))
        sloped = jnp.concatenate([slopes[b, 2 * c], slopes[b, 2 * c + 1]], axis=1)
        parts = []
        for k in range(PROBES):
            level = corr[b, k * ROWS : (k + 1) * ROWS]
            level = jnp.concatenate([level] * (2 * CHUNK // WIDTH), axis=1)
            parts.append(
                (sloped * (aligned[k * ROWS : (k + 1) * ROWS] - level)).astype(BF16)
            )
        grad[b] += nn(jnp.concatenate(parts, axis=0), two(keys_of, c))

    def second_block(b, carry):
        def step(c, carry):
            second_pass(b, c)
            return carry

        last = last_chunk(b)

        @pl.when(last % 2 == 0)
        def _():
            slopes[b, last + 1] = jnp.zeros((ROWS, CHUNK), F32)

        return lax.fori_loop(0, last // 2 + 1, step, carry)

    lax.fori_loop(0, 2, second_block, 0)

    wbuf[...] = jnp.zeros((LANES, WIDTH), F32)
    both = jnp.concatenate([lr[0], lr[1]], axis=1)
    for k in range(PROBES):
        stack = jnp.concatenate(
            [
                grad[b, k * ROWS : (k + 1) * ROWS] * inv[b] for b in range(2)
            ],
            axis=0,
        )
        wbuf[pl.ds(pl.multiple_of(k * 32 + head * 16, 16), RANK), :] = nn(
            both, stack, HIGHEST
        )
    turned = wbuf[...].T
    for i in range(SEQ):
        w_out[i] = turned[4 * i : 4 * i + 4]
    w_in[s] = w_out[s]
    send_seq(lambda to: w_out.at[to], w_in, 4)

    arrived(h_in, 3)
    piece = total(h_in)
    e_out[...] = piece
    e_in[s] = piece
    send_seq(lambda to: e_out, e_in, 5)

    arrived(w_in, 4)
    masked, repeated = spread(total(w_in))
    srep[KNOWN : KNOWN + PROBES] = repeated
    dots = nt(masked, srep[...], HIGHEST) * (1.0 / (RANK * 2 * tensor * WIDTH))
    c_out[...] = dots
    c_in[s] = dots
    send_seq(lambda to: c_out, c_in, 6)

    arrived(e_in, 5)
    gmat[...] = jnp.concatenate([e_in[i] for i in range(SEQ)], axis=0)
    gfull = gmat[...]
    eye = (iota((LANES, LANES), 0) == iota((LANES, LANES), 1)).astype(F32)
    square = nn(gfull, gfull, HIGHEST)
    cube = nn(square, gfull, HIGHEST)
    once = 2.0 * eye - gfull
    twice = 4.0 * (eye + square) - 6.0 * gfull - cube

    arrived(c_in, 6)
    piece = total(c_in)
    d_out[...] = piece
    d_in[t] = piece
    send_tensor(d_out, d_in, 7)
    arrived(d_in, 7)
    dots = total(d_in)

    lane = iota((PROBES, LANES), 1)
    known = jnp.where(lane < KNOWN, dots, 0.0)
    coeff = nn(known, once, HIGHEST)
    quad = nn(known, twice, HIGHEST)
    pick = (lane == iota((PROBES, LANES), 0) + NB).astype(F32)
    small = nt(jnp.concatenate([quad, pick], axis=0), known, HIGHEST)
    gram = dots[:, KNOWN : KNOWN + PROBES] - small[0:PROBES]
    out_ref[4:8] = jnp.concatenate(
        [small[PROBES:], jnp.zeros((PROBES, LANES - PROBES), F32)], axis=1
    )

    low = [[None] * PROBES for _ in range(PROBES)]
    for j in range(PROBES):
        pivot = gram[j : j + 1, j : j + 1]
        for m in range(j):
            pivot = pivot - low[j][m] * low[j][m]
        low[j][j] = jnp.sqrt(pivot)
        for i in range(j + 1, PROBES):
            entry = gram[i : i + 1, j : j + 1]
            for m in range(j):
                entry = entry - low[i][m] * low[j][m]
            low[i][j] = entry / low[j][j]
    row4, col4 = iota((PROBES, LANES), 0), iota((PROBES, LANES), 1)
    upper = jnp.zeros((PROBES, LANES), F32)
    for i in range(PROBES):
        for j in range(i + 1):
            upper = jnp.where((row4 == j) & (col4 == i), low[i][j], upper)
    out_ref[8:12] = upper

    mix = jnp.where(
        lane < KNOWN,
        -coeff,
        (lane == iota((PROBES, LANES), 0) + KNOWN).astype(F32),
    )
    residue = nn(mix, srep[...], HIGHEST)
    rows = []
    for i in range(PROBES):
        row = residue[i : i + 1]
        for m in range(i):
            row = row - low[i][m] * rows[m]
        rows.append(row / low[i][i])
    lane1 = iota((1, LANES), 1) // 32
    made = []
    for d in range(4):
        row = rows[0][:, d * LANES : (d + 1) * LANES]
        for k in range(1, PROBES):
            row = jnp.where(lane1 == k, rows[k][:, d * LANES : (d + 1) * LANES], row)
        made.append(row)
    out_ref[0:4] = jnp.concatenate(made, axis=0)

    shards = kv.at[pl.ds(0, SEQ - 1)]
    pltpu.make_async_copy(shards, shards, kv_send).wait()
    q_copy.wait_send()
    lr_copy.wait_send()
    for n, into in enumerate((lr_in, vt_in, g_in, h_in, w_in, e_in, c_in, d_in)):
        sent(into, n)


def unpack(packed, next_ref, diag_ref, sub_ref):
    for k in range(PROBES):
        for h in range(2):
            at = k * 32 + h * 16
            next_ref[k, h] = packed[0:4, at : at + 16]
    diag_ref[0] = packed[4:8, 0:PROBES]
    sub_ref[0] = packed[8:12, 0:PROBES]


def on_device(
    activations, adapter_down_weight, queries, keys, values, sequence_lengths, probe, basis
):
    tensor = lax.axis_size("tensor")
    width = activations.shape[2]
    act = activations.reshape(ROWS, width).T
    down = adapter_down_weight.T
    q = queries.reshape(2 * ROWS, WIDTH)
    k = keys.reshape(ROWS, WIDTH)
    v = values.reshape(ROWS, WIDTH)
    probe_in = probe.transpose(0, 2, 3, 1)
    basis_in = basis.transpose(1, 2, 3, 0).reshape(LANES, NB)
    anywhere = pl.BlockSpec(memory_space=pl.ANY)
    in_vmem = pl.BlockSpec(memory_space=pltpu.VMEM)
    piece = (4, LANES)
    by_seq = pltpu.VMEM((SEQ,) + piece, F32)
    by_tensor = pltpu.VMEM((tensor,) + piece, F32)
    one = pltpu.VMEM(piece, F32)
    packed = pl.pallas_call(
        functools.partial(kernel, tensor),
        out_shape=jax.ShapeDtypeStruct((16, LANES), F32),
        in_specs=[anywhere] * 5
        + [pl.BlockSpec(memory_space=pltpu.SMEM)]
        + [anywhere] * 2,
        out_specs=in_vmem,
        scratch_shapes=[
            pltpu.VMEM((width, ROWS), BF16),
            pltpu.VMEM((RANK, width), BF16),
            pltpu.VMEM((2 * ROWS, WIDTH), BF16),
            pltpu.VMEM((2 * ROWS, WIDTH), F32),
            pltpu.VMEM((3, ROWS, WIDTH), BF16),
            pltpu.VMEM((PROBES, 2, 4, RANK), F32),
            pltpu.VMEM((LANES, NB), F32),
            pltpu.VMEM((SEQ, 2, ROWS, WIDTH), BF16),
            pltpu.VMEM((2, GROUPS, (PROBES + 1) * GROUP, WIDTH), BF16),
            pltpu.VMEM((2, GROUPS, (PROBES + 2) * GROUP, 2 * WIDTH), F32),
            pltpu.VMEM((2, CHUNKS, ROWS, CHUNK), F32),
            pltpu.VMEM((2, PROBES * ROWS, WIDTH), BF16),
            pltpu.VMEM((2, PROBES * ROWS, WIDTH), F32),
            pltpu.VMEM((2, ROWS, WIDTH), F32),
            pltpu.VMEM((2, PROBES * ROWS, WIDTH), F32),
            pltpu.VMEM((LANES, WIDTH), F32),
            pltpu.VMEM((LANES, WIDTH), F32),
            pltpu.VMEM((LANES, 4 * LANES), F32),
            pltpu.VMEM((LANES, LANES), F32),
            pltpu.VMEM((RANK, ROWS), F32),
            pltpu.VMEM((tensor, RANK, ROWS), F32),
            pltpu.VMEM((2, RANK, ROWS), F32),
            one,
            by_seq,
            by_seq,
            by_seq,
            one,
            by_seq,
            one,
            by_tensor,
            by_seq,
            by_seq,
            one,
            by_tensor,
            one,
            by_seq,
            pltpu.SemaphoreType.DMA((7,)),
            pltpu.SemaphoreType.DMA,
            pltpu.SemaphoreType.DMA((6,)),
            pltpu.SemaphoreType.DMA((4, 6)),
            pltpu.SemaphoreType.DMA((4, 4, 2)),
            pltpu.SemaphoreType.DMA((2,)),
            pltpu.SemaphoreType.DMA((2,)),
            pltpu.SemaphoreType.DMA((8,)),
            pltpu.SemaphoreType.DMA((8,)),
        ],
        compiler_params=pltpu.CompilerParams(
            collective_id=0, has_side_effects=True, vmem_limit_bytes=60 * 1024 * 1024
        ),
    )(act, down, q, k, v, sequence_lengths, probe_in, basis_in)
    turned, diag, sub = pl.pallas_call(
        unpack,
        out_shape=(
            jax.ShapeDtypeStruct((PROBES, 2, 4, RANK), F32),
            jax.ShapeDtypeStruct((1, PROBES, PROBES), F32),
            jax.ShapeDtypeStruct((1, PROBES, PROBES), F32),
        ),
        in_specs=[in_vmem],
        out_specs=(in_vmem,) * 3,
    )(packed)
    return turned.transpose(0, 3, 1, 2)[None], diag, sub


def solution(mesh):
    in_specs = (
        P(None, "seq", "tensor"),
        P("tensor", None),
        P(None, "seq", "tensor", None),
        P(None, "seq", "tensor", None),
        P(None, "seq", "tensor", None),
        P(),
        P(None, None, "tensor", "seq"),
        P(None, None, "tensor", "seq"),
    )
    out_specs = (P(None, None, None, "tensor", "seq"), P(), P())
    return jax.shard_map(
        on_device, mesh=mesh, in_specs=in_specs, out_specs=out_specs, check_vma=False
    )
```
